512 devices in a mesh: ap: 128 (over z_hi, y, x), sec: 4 (over z_lo, core).
Axes of the slice: x: 4, y: 8, z: 8 (z_hi: 4, z_lo: 2; z = z_hi * 2 + z_lo), core: 2. Of those that a mesh axis runs over, the one named last changes fastest.
Arguments:
- polar: bfloat16 [128, 2, 2048, 1024], P('ap', None, 'sec'), may hold values from -128 to 128
- autofocus: float32 [2, 2, 128, 1024], P(None, None, 'ap'), may hold values from -3.140625 to 3.140625
- offsets: int32 [2, 2, 128, 2048], P(None, None, 'ap', 'sec'), may hold values from 0 to 504, as said below
- weights: float32 [2, 2, 128, 8, 2048], P(None, None, 'ap', None, 'sec'), may hold values from -2.4 to 2.4
Outputs:
- merged: bfloat16 [128, 2, 2048, 1024], P('ap', None, 'sec')
The draws below stay inside these ranges and needn't reach their ends.
Inputs may be any that keep to these rules, and one draw needn't show every extreme that they name: `offsets`: for target s at section k, with b the bit k of s, every offset lies from b * (248) to b * 248 + 512 // 2 + 8 - 8.
All inputs are finite; a program needn't handle non-finite values.
Results may differ from the reference program's by a relative error of at most 0.007.
Values may be sent and summed in bfloat16 or wider, within the bound.
No kernel may reach another device: no remote copies, remote signals or barrier semaphores. Data moves between devices by JAX's collectives and lax.ppermute only.
A program may use at most 64 MiB of HBM per device.

```python
import jax
import jax.numpy as jnp
from jax import lax

RANGE = 1024
BEAM_DEV = 512
TAPS = 8
MARGIN = 8
SECTIONS = 2
SUBS = 128
BEAMS = 2048
N_SEC = 4


def draw_polar(key, part):
    key = jax.random.fold_in(key, 11)
    keys = jax.random.split(key, 3)
    beam_place = jnp.arange(BEAMS, dtype=jnp.float32) / BEAMS
    sub_scale = jax.random.uniform(keys[0], (SUBS, 1, 1, 1), jnp.float32, 0.0, 1.0)
    jitter = jax.random.uniform(keys[1], (SUBS, 1, BEAMS, 1), jnp.float32, -0.30103, 0.0)
    noise = jax.random.truncated_normal(keys[2], -4.0, 4.0, (SUBS, 2, BEAMS, RANGE), jnp.float32)
    ramp = 0.5 * beam_place
    scale = 10.0 ** (sub_scale + jitter + ramp[None, None, :, None])
    return (noise * scale).astype(jnp.bfloat16)


def draw_offsets(key, part):
    key = jax.random.fold_in(key, 23)
    level_index = jnp.arange(SECTIONS, dtype=jnp.int32)[:, None, None, None]
    sub_index = jnp.arange(SUBS, dtype=jnp.int32)[None, None, :, None]
    beam_local = (jnp.arange(BEAMS, dtype=jnp.int32) % BEAM_DEV)[None, None, None, :]
    half_index = jnp.right_shift(sub_index, level_index) % 2
    lower = half_index * (BEAM_DEV // 2 - MARGIN)
    reach = BEAM_DEV // 2 + MARGIN - TAPS
    base_rows = lower + beam_local * reach // (BEAM_DEV - 1)
    jitter = jax.random.randint(key, (SECTIONS, 2, SUBS, BEAMS), -2, 3, dtype=jnp.int32)
    moved = jnp.clip(base_rows + jitter, lower, lower + reach)
    edges = (beam_local == 0) | (beam_local == BEAM_DEV - 1)
    return jnp.where(edges, base_rows, moved).astype(jnp.int32)


def level_of(rng, shape, cuts, least, top_value):
    loudness, own = 1.0, jax.random.fold_in(rng, 6)
    for axis_at, blocks in cuts:
        heights = jnp.exp(jax.random.uniform(jax.random.fold_in(own, axis_at), (blocks,), jnp.float32, least / len(cuts), top_value / len(cuts)))
        loudness = loudness * jnp.repeat(heights, shape[axis_at] // blocks).reshape([-1 if axis == axis_at else 1 for axis in range(len(shape))])
    return loudness


def centred(own_key, shape, width, most, cuts=(), kind=jnp.bfloat16):
    entries = width * jax.random.normal(own_key, shape, jnp.float32)
    if cuts:
        entries = entries * level_of(own_key, shape, cuts, -0.22, 0.18)
    return jnp.clip(entries, -most, most).astype(kind)


def setup_inputs(seed: int = 0) -> dict:
    key_of = jax.random.split(jax.random.key(seed), 5)
    polar = draw_polar(jax.random.fold_in(key_of[4], 71), 0)
    autofocus = jnp.clip(jax.random.uniform(key_of[1], (SECTIONS, 2, SUBS, RANGE), jnp.float32, -3.140625, 3.140625), -3.140625, 3.140625)
    offsets = draw_offsets(jax.random.fold_in(key_of[4], 71), 0)
    weights = centred(key_of[3], (SECTIONS, 2, SUBS, TAPS, BEAMS), 0.4, 2.4, ((2, 128), (4, 4)), jnp.float32)
    return dict(polar=polar, autofocus=autofocus, offsets=offsets, weights=weights)


def pick_rows(block_rows, row_index):
    return block_rows[row_index]

def merge_level(picture, autofocus, offsets, weights, merge_step):
    partner_gap = 2 ** merge_step

    def one_target(target):
        low_index = target - target // partner_gap % 2 * partner_gap
        real_part = jnp.zeros((N_SEC, BEAM_DEV, RANGE), jnp.float32)
        imag_part = jnp.zeros((N_SEC, BEAM_DEV, RANGE), jnp.float32)
        for child_index in range(2):
            source = lax.dynamic_index_in_dim(picture, low_index + child_index * partner_gap, 0, keepdims=False)
            source = source.astype(jnp.float32).reshape(2, N_SEC, BEAM_DEV, RANGE).transpose(1, 2, 0, 3)
            offset_rows = lax.dynamic_index_in_dim(offsets[merge_step, child_index], target, 0, keepdims=False)
            offset_rows = offset_rows.reshape(N_SEC, BEAM_DEV).astype(jnp.int32)
            tap_weights = lax.dynamic_index_in_dim(weights[merge_step, child_index], target, 0, keepdims=False)
            tap_weights = lax.optimization_barrier(tap_weights.astype(jnp.bfloat16)).astype(jnp.float32)
            tap_weights = tap_weights.reshape(TAPS, N_SEC, BEAM_DEV)
            gathered = jnp.zeros((N_SEC, BEAM_DEV, 2, RANGE), jnp.float32)
            for tap_index in range(TAPS):
                picked = jax.vmap(pick_rows)(source, offset_rows + tap_index)
                gathered = gathered + tap_weights[tap_index][:, :, None, None] * picked
            phase_turn = lax.dynamic_index_in_dim(autofocus[merge_step, child_index], target, 0, keepdims=False)
            cosine = jnp.cos(phase_turn)
            sine_part = jnp.sin(phase_turn)
            real_part = real_part + (cosine * gathered[:, :, 0] - sine_part * gathered[:, :, 1])
            imag_part = imag_part + (sine_part * gathered[:, :, 0] + cosine * gathered[:, :, 1])
        merged = jnp.stack([real_part, imag_part]).reshape(2, N_SEC * BEAM_DEV, RANGE)
        return merged.astype(jnp.bfloat16)
    return lax.map(one_target, jnp.arange(picture.shape[0], dtype=jnp.int32))

def reference(polar, autofocus, offsets, weights):
    energy_sum = lax.optimization_barrier(jnp.sum(jnp.square(polar.astype(jnp.float32)), axis=(1, 2, 3)))
    energy_gain = lax.rsqrt(energy_sum / (RANGE * BEAMS) + 1e-06)
    picture = (polar.astype(jnp.float32) * energy_gain[:, None, None, None]).astype(jnp.bfloat16)
    for merge_step in range(SECTIONS):
        picture = merge_level(picture, autofocus, offsets, weights, merge_step)
    return picture
```

```python
import functools

import jax
import jax.numpy as jnp
from jax import lax
from jax.experimental import pallas as pl
from jax.experimental.pallas import tpu as pltpu
from jax.sharding import Mesh
from jax.sharding import PartitionSpec as P

GROUP = 4
TILE = 8
STEP = 31
SPAN = 33
BAND = SPAN * TILE
BULK = 256
TAPS = 8
LANES = 128
BLOCK = 256
OUT_ROWS = 256
FAR_PARTS = (768, 256)
NEAR_PARTS = (512, 256, 256)
DATA_TILES = 8
PIECES = 4
TERMS = 3


def partner(value, flip):
    return lax.ppermute(value, "x", [(i, i ^ flip) for i in range(GROUP)])


def terms_of(value):
    terms = []
    for _ in range(TERMS):
        terms.append(value.astype(jnp.bfloat16).astype(jnp.float32))
        value = value - terms[-1]
    return terms


def place_bits():
    place = lax.axis_index("x")
    return place % 2, place // 2


def encode(tail, bit, weights, offsets, phases):
    beams = weights.shape[-1]
    own = bit == 0
    starts, angles = [], []
    for child in range(2):
        lanes = slice(child * beams, (child + 1) * beams)
        taps = jnp.where(own, weights[child, 0], weights[1 - child, 0])
        tail[0, :, lanes] = taps.astype(jnp.bfloat16)
        start = jnp.where(own, offsets[child], offsets[1 - child]) - bit * (STEP * TILE)
        starts.append(start.astype(jnp.float32))
        angles += terms_of(jnp.where(own, phases[child], phases[1 - child]))
    rows = [jnp.concatenate(starts, axis=1)] + angles
    rows.append(jnp.zeros((TILE - len(rows), 2 * beams), jnp.float32))
    tail[1] = jnp.concatenate(rows).astype(jnp.bfloat16)


def decode(data):
    if data.shape[0] == 2:
        return data[0].astype(jnp.float32), data[1].astype(jnp.float32)
    at, each = 2 * SPAN + 1, DATA_TILES // 2
    return [
        jnp.concatenate([data[at + i * each + k].astype(jnp.float32) for k in range(each)], axis=1) for i in range(2)
    ]


def section_specs(section, *arrays):
    def spec(shape):
        return pl.BlockSpec((1, *shape[1:]), lambda i: (section,) + (0,) * (len(shape) - 1))

    return [spec(array.shape) for array in arrays]


def prepare_kernel(*refs):
    low, high = place_bits()
    sections, rows = (refs[0:3], refs[3:6]), refs[6]
    far, *near, energy, near_data, last_data, image, sems = refs[7:]
    piece = image.shape[1] // PIECES
    loads = []
    for k in range(PIECES):
        some = pl.ds(k * piece, piece)
        loads.append(pltpu.make_async_copy(rows.at[:, some], image.at[:, some], sems.at[k]))
        loads[-1].start()
    for data, bit, section in zip((near_data, last_data), (low, high), sections):
        encode(data, bit, *(array.at[0] for array in section))
    width, each = far.shape[-1], DATA_TILES // 2
    for i in range(2):
        for k in range(each):
            far[2 * SPAN + 1 + i * each + k] = near_data[i, :, k * width : (k + 1) * width]

    def add(i, total):
        block = image[:, pl.ds(i * 4, 4)].astype(jnp.float32)
        return total + jnp.sum(block * block, axis=(0, 1))

    total = jnp.zeros(image.shape[2:], jnp.float32)
    for k in range(PIECES):
        loads[k].wait()
        total = lax.fori_loop(k * piece // 4, (k + 1) * piece // 4, add, total)
    energy[...] = jnp.broadcast_to(jnp.sum(total, keepdims=True), energy.shape)
    for half in range(2):
        place = slice(half * SPAN, (half + 1) * SPAN)
        far[place] = image[half, pl.ds(low * STEP, SPAN), :, FAR_PARTS[0] :]
        at = 0
        for part in near:
            width = part.shape[-1]
            part[place] = image[half, pl.ds((1 - low) * STEP, SPAN), :, at : at + width]
            at += width


def prepare(rows, section):
    bins = rows.shape[-1]
    sizes = [(2 * SPAN + 1 + DATA_TILES, FAR_PARTS[1])] + [(2 * SPAN + (i == 0), w) for i, w in enumerate(NEAR_PARTS)]
    shapes = [jax.ShapeDtypeStruct((tiles, TILE, w), rows.dtype) for tiles, w in sizes]
    shapes.append(jax.ShapeDtypeStruct((1, LANES), jnp.float32))
    shapes += [jax.ShapeDtypeStruct((2, TILE, bins), rows.dtype)] * 2
    return pl.pallas_call(
        prepare_kernel,
        grid=(1,),
        out_shape=shapes,
        in_specs=[*section_specs(0, *section), *section_specs(1, *section), pl.BlockSpec(memory_space=pl.ANY)],
        out_specs=[pl.BlockSpec(memory_space=pltpu.VMEM)] * len(shapes),
        scratch_shapes=[pltpu.VMEM(rows.shape, rows.dtype), pltpu.SemaphoreType.DMA((PIECES,))],
        compiler_params=pltpu.CompilerParams(vmem_limit_bytes=52 * 2**20),
        cost_estimate=pl.CostEstimate(flops=4 * SPAN * TILE * bins, bytes_accessed=4_000_000, transcendentals=0),
        name="prepare",
    )(*section, *section, rows)


def seal_kernel(far, near, energy, far_result, near_result, tail, sems):
    row = lax.broadcasted_iota(jnp.int32, (TILE, LANES), 0)
    value = jnp.zeros((TILE, LANES), jnp.float32)
    for i, term in enumerate(terms_of(energy[...])):
        value = jnp.where(row == i, term, value)
    tail[0] = value.astype(jnp.bfloat16)
    copies = [
        pltpu.make_async_copy(tail, result.at[pl.ds(2 * SPAN, 1), :, 0:LANES], sems.at[i])
        for i, result in enumerate((far_result, near_result))
    ]
    for copy in copies:
        copy.start()
    for copy in copies:
        copy.wait()


def seal(far, near, energy):
    anywhere = pl.BlockSpec(memory_space=pl.ANY)
    return pl.pallas_call(
        seal_kernel,
        out_shape=[jax.ShapeDtypeStruct(part.shape, part.dtype) for part in (far, near)],
        in_specs=[anywhere, anywhere, pl.BlockSpec(memory_space=pltpu.VMEM)],
        out_specs=[anywhere, anywhere],
        scratch_shapes=[pltpu.VMEM((1, TILE, LANES), far.dtype), pltpu.SemaphoreType.DMA((2,))],
        input_output_aliases={0: 0, 1: 1},
        compiler_params=pltpu.CompilerParams(vmem_limit_bytes=4 * 2**20),
        cost_estimate=pl.CostEstimate(flops=10_000, bytes_accessed=20_000, transcendentals=0),
        name="seal",
    )(far, near, energy)


def build_table(target, columns, first_row, row_tiles, group):
    rows = group * TILE
    lane = lax.broadcasted_iota(jnp.int32, (rows, LANES), 1)

    def step(i, carry):
        block = columns[pl.ds(pl.multiple_of(first_row + i * rows, TILE), rows), :]
        place = pl.ds(pl.multiple_of(i * rows, TILE), rows)

        def spread(column):
            return jnp.broadcast_to(block[:, column : column + 1], (rows, LANES))

        rest = jnp.zeros((rows, LANES), jnp.float32)
        for child in range(2):
            start = spread(2 * TAPS + child).astype(jnp.int32)
            taps = [spread(child * TAPS + t) for t in range(TAPS)]

            def entries(source, part):
                hit = source - start
                for t in range(TAPS):
                    part = jnp.where(hit == t, taps[t], part)
                return part

            for part in range(BULK // LANES):
                at = child * BULK + part * LANES
                target[place, at : at + LANES] = entries(lane + part * LANES, jnp.zeros((rows, LANES), jnp.float32))
            inside = (lane >= child * TILE) & (lane < (child + 1) * TILE)
            rest = entries(jnp.where(inside, lane + (BULK - child * TILE), -TAPS), rest)
        target[place, 2 * BULK : 2 * BAND] = rest[:, : 2 * TILE]
        return carry

    lax.fori_loop(0, row_tiles // group, step, 0)


def table_kernel(data, table, turn, columns):
    beams = columns.shape[0]
    taps, rest = decode(data)
    starts = jnp.concatenate([rest[:1, :beams], rest[:1, beams:], jnp.zeros((TILE - 2, beams), jnp.float32)])
    fill = jnp.zeros((LANES - 2 * TAPS - TILE, beams), jnp.float32)
    columns[...] = jnp.transpose(jnp.concatenate([taps[:, :beams], taps[:, beams:], starts, fill]))
    for child in range(2):
        at = 1 + child * TERMS
        phase = rest[at : at + 1] + rest[at + 1 : at + 2] + rest[at + 2 : at + 3]
        turn[2 * child : 2 * child + 1, :] = jnp.cos(phase)
        turn[2 * child + 1 : 2 * child + 2, :] = jnp.sin(phase)
    first_row = place_bits()[1] * (STEP * TILE) if table.shape[0] == BAND else 0
    row_tiles = table.shape[0] // TILE
    build_table(table, columns, first_row, row_tiles, 3 if row_tiles % 3 == 0 else 4)


def make_table(rows, data, beams):
    whole = pl.BlockSpec(memory_space=pltpu.VMEM)
    table, turn = pl.pallas_call(
        table_kernel,
        out_shape=[jax.ShapeDtypeStruct(s, jnp.float32) for s in ((rows, 2 * BAND), (4, 2 * beams))],
        in_specs=[whole],
        out_specs=[whole] * 2,
        scratch_shapes=[pltpu.VMEM((beams, LANES), jnp.float32)],
        compiler_params=pltpu.CompilerParams(vmem_limit_bytes=8 * 2**20),
        cost_estimate=pl.CostEstimate(flops=rows * 12_000, bytes_accessed=rows * 4096, transcendentals=8192),
        name="table",
    )(data)
    return table.astype(jnp.bfloat16), turn


def turned(real, imag, cosine, sine):
    return cosine * real - sine * imag, sine * real + cosine * imag


def joined(left, right):
    both = []
    for a, b in zip(left, right):
        both.append(jnp.concatenate([a[:BULK], b[:BULK], a[BULK:], b[BULK:]]).astype(jnp.bfloat16))
    return jnp.concatenate(both, axis=1)


def first_merges(images, tables, turns, gains):
    width = images[1].shape[-1]

    def child(source, turn, row, gain):
        real, imag = (
            source[half * SPAN : (half + 1) * SPAN].astype(jnp.float32).reshape(BAND, width) for half in range(2)
        )
        scale = jnp.concatenate([gain] * (width // LANES), axis=1)
        return turned(real, imag, scale * turn[row : row + 1, :], scale * turn[row + 1 : row + 2, :])

    def merge(left, right, table):
        merged = jnp.dot(table[...], joined(left, right), preferred_element_type=jnp.float32)
        return merged[:, :width], merged[:, width:]

    own, one, two, three = images
    near_turn, far_turn, last_turn = turns
    near = merge(child(own, near_turn, 0, gains[0:1]), child(one, near_turn, 2, gains[1:2]), tables[0])
    near = turned(*near, last_turn[0:1, :], last_turn[1:2, :])
    far = merge(child(two, far_turn, 0, gains[2:3]), child(three, far_turn, 2, gains[3:4]), tables[1])
    far = turned(*far, last_turn[2:3, :], last_turn[3:4, :])
    return joined(near, far)


def merge_kernel(cells, *refs):
    images, tables, turns, energies = refs[0:4], refs[4:7], refs[7:10], refs[10:14]
    result, gains = refs[14:16]

    def unsealed(tail):
        terms = tail[0].astype(jnp.float32)
        return terms[0:1] + terms[1:2] + terms[2:3]

    energy = jnp.concatenate([energies[0][...]] + [unsealed(tail) for tail in energies[1:]])
    gains[...] = lax.rsqrt(energy / cells + 1e-06)
    both = first_merges(images, tables, turns, gains[...])
    merged = jnp.dot(tables[2][...], both, preferred_element_type=jnp.float32)
    width = result.shape[-1]
    result[0, 0] = merged[:, :width].astype(jnp.bfloat16)
    result[0, 1] = merged[:, width:].astype(jnp.bfloat16)


def merge_cost(width, beams):
    flops = 8 * width * BAND * (2 * BAND + beams)
    return pl.CostEstimate(flops=flops, bytes_accessed=8192 * width, transcendentals=0)


def merge_first(images, tables, turns, energy, tails, cells, shape):
    width = images[1].shape[-1]
    beams = shape[2]
    in_specs = [pl.BlockSpec((image.shape[0], TILE, BLOCK), lambda i: (0, 0, i)) for image in images]
    in_specs += [pl.BlockSpec(t.shape, lambda i: (0, 0)) for t in tables]
    in_specs += [pl.BlockSpec((t.shape[0], BLOCK), lambda i: (0, i)) for t in turns]
    in_specs += [pl.BlockSpec((1, LANES), lambda i: (0, 0))]
    in_specs += [pl.BlockSpec((1, TILE, LANES), lambda i: (2 * SPAN, 0, 0)) for tail in tails]
    return pl.pallas_call(
        functools.partial(merge_kernel, cells),
        grid=(width // BLOCK,),
        out_shape=[jax.ShapeDtypeStruct(shape, jnp.bfloat16), jax.ShapeDtypeStruct((GROUP, LANES), jnp.float32)],
        in_specs=in_specs,
        out_specs=[
            pl.BlockSpec((1, 2, beams, BLOCK), lambda i: (0, 0, 0, i)),
            pl.BlockSpec((GROUP, LANES), lambda i: (0, 0)),
        ],
        compiler_params=pltpu.CompilerParams(vmem_limit_bytes=16 * 2**20),
        cost_estimate=merge_cost(width, beams),
        name="merge",
    )(*images, *tables, *turns, energy, *tails)


def finish_kernel(at, skip, *refs):
    images, tables, turns, gains = refs[0:4], refs[4:7], refs[7:10], refs[10]
    result, buffer, sems = refs[12:15]
    width = buffer.shape[-1]
    bins = slice(at, at + width)
    own, one, two, three = images
    cut = [own[:, :, skip : skip + width], one[...], two[:, :, skip : skip + width], three[...]]
    both = first_merges(cut, tables, [turn[:, bins] for turn in turns], gains[...])
    copies = []
    for k, row in enumerate(range(0, buffer.shape[1], OUT_ROWS)):
        rows = slice(row, row + OUT_ROWS)
        merged = jnp.dot(tables[2][rows, :], both, preferred_element_type=jnp.float32)
        for half in range(2):
            buffer[half, rows] = merged[:, half * width : (half + 1) * width].astype(jnp.bfloat16)
        copies.append(pltpu.make_async_copy(buffer.at[:, rows], result.at[0, :, rows, bins], sems.at[k]))
        copies[-1].start()
    for copy in copies:
        copy.wait()


def finish(prior, at, images, tables, turns, gains):
    width = images[1].shape[-1]
    beams = prior.shape[2]
    operands = [*images, *tables, *turns, gains]
    return pl.pallas_call(
        functools.partial(finish_kernel, at, at % FAR_PARTS[0]),
        out_shape=jax.ShapeDtypeStruct(prior.shape, prior.dtype),
        in_specs=[pl.BlockSpec(memory_space=pltpu.VMEM)] * len(operands) + [pl.BlockSpec(memory_space=pl.ANY)],
        out_specs=pl.BlockSpec(memory_space=pl.ANY),
        scratch_shapes=[pltpu.VMEM((2, beams, width), prior.dtype), pltpu.SemaphoreType.DMA((beams // OUT_ROWS,))],
        input_output_aliases={len(operands): 0},
        compiler_params=pltpu.CompilerParams(vmem_limit_bytes=16 * 2**20),
        cost_estimate=merge_cost(width, beams),
        name="finish",
    )(*operands, prior)


def shards(polar, autofocus, offsets, weights):
    beams, bins = polar.shape[2], polar.shape[3]
    cells = 2 * beams * lax.axis_size("sec") * bins // 2
    rows = polar.reshape(2, beams // TILE, TILE, bins)
    low, _ = place_bits()

    first = lax.dynamic_slice(rows, (0, low * STEP, 0, 0), (2, SPAN, TILE, FAR_PARTS[0]))
    first = first.reshape(2 * SPAN, TILE, FAR_PARTS[0])
    far = [partner(first, 2)]
    rows, first = lax.optimization_barrier((rows, first))
    second, *near, energy, near_data, last_data = prepare(rows, (weights, offsets, autofocus))
    energy = lax.psum(energy, "sec")
    second, near[0] = seal(second, near[0], energy)
    far.append(partner(second, 2))
    near_table, near_turn = make_table(BAND, near_data, beams)
    last_table, last_turn = make_table(beams, last_data, beams)
    near[1], far[0], near_table, last_table = lax.optimization_barrier((near[1], far[0], near_table, last_table))
    one, three = ([partner(part, flip) for part in near[:2]] for flip in (1, 3))
    near[2], one[0], three[0] = lax.optimization_barrier((near[2], one[0], three[0]))
    one.append(partner(near[2], 1))
    three.append(partner(near[2], 3))
    far_table, far_turn = make_table(BAND, far[1], beams)

    tables = [near_table, far_table, last_table]
    turns = [near_turn, far_turn, last_turn]
    own = [first, second]
    images = [first, one[0], far[0], three[0]]
    merged, gains = merge_first(images, tables, turns, energy, [one[0], far[1], three[0]], cells, polar.shape)
    at = NEAR_PARTS[0]
    for i in (1, 2):
        k = at // FAR_PARTS[0]
        merged = finish(merged, at, [own[k], one[i], far[k], three[i]], tables, turns, gains)
        at += NEAR_PARTS[i]
    return merged


def solution(mesh):
    ring = Mesh(mesh.devices.reshape(-1, GROUP, mesh.devices.shape[1]), ("rest", "x", "sec"))
    placed = (
        P(("rest", "x"), None, "sec", None),
        P(None, None, ("rest", "x"), None),
        P(None, None, ("rest", "x"), "sec"),
        P(None, None, ("rest", "x"), None, "sec"),
    )
    return jax.shard_map(
        shards, mesh=ring, in_specs=placed, out_specs=P(("rest", "x"), None, "sec", None), check_vma=False
    )
```

```python
import functools

import jax
import jax.numpy as jnp
from jax import lax
from jax.experimental import pallas as pl
from jax.experimental.pallas import tpu as pltpu
from jax.sharding import Mesh
from jax.sharding import PartitionSpec as P

GROUP = 4
TILE = 8
STEP = 31
SPAN = 33
BAND = SPAN * TILE
BULK = 256
TAPS = 8
LANES = 128
BLOCK = 256
OUT_ROWS = 256
FAR_PARTS = (768, 256)
NEAR_PARTS = (768, 256)
DATA_TILES = 8
PIECES = 4
TERMS = 3


def partner(value, flip):
    return lax.ppermute(value, "x", [(i, i ^ flip) for i in range(GROUP)])


def terms_of(value):
    terms = []
    for _ in range(TERMS):
        terms.append(value.astype(jnp.bfloat16).astype(jnp.float32))
        value = value - terms[-1]
    return terms


def place_bits():
    place = lax.axis_index("x")
    return place % 2, place // 2


def encode(tail, bit, weights, offsets, phases):
    beams = weights.shape[-1]
    own = bit == 0
    starts, angles = [], []
    for child in range(2):
        lanes = slice(child * beams, (child + 1) * beams)
        taps = jnp.where(own, weights[child, 0], weights[1 - child, 0])
        tail[0, :, lanes] = taps.astype(jnp.bfloat16)
        start = jnp.where(own, offsets[child], offsets[1 - child]) - bit * (STEP * TILE)
        starts.append(start.astype(jnp.float32))
        angles += terms_of(jnp.where(own, phases[child], phases[1 - child]))
    rows = [jnp.concatenate(starts, axis=1)] + angles
    rows.append(jnp.zeros((TILE - len(rows), 2 * beams), jnp.float32))
    tail[1] = jnp.concatenate(rows).astype(jnp.bfloat16)


def decode(data):
    if data.shape[0] == 2:
        return data[0].astype(jnp.float32), data[1].astype(jnp.float32)
    at, each = 2 * SPAN + 1, DATA_TILES // 2
    return [
        jnp.concatenate([data[at + i * each + k].astype(jnp.float32) for k in range(each)], axis=1) for i in range(2)
    ]


def cut_kernel(rows, result, sems):
    low, _ = place_bits()
    copies = []
    for half in range(2):
        for i in range(PIECES):
            at, end = SPAN * i // PIECES, SPAN * (i + 1) // PIECES
            source = rows.at[half, pl.ds(low * STEP + at, end - at), :, 0 : result.shape[-1]]
            target = result.at[pl.ds(half * SPAN + at, end - at)]
            copies.append(pltpu.make_async_copy(source, target, sems.at[len(copies)]))
            copies[-1].start()
    for copy in copies:
        copy.wait()


def cut(rows):
    return pl.pallas_call(
        cut_kernel,
        out_shape=jax.ShapeDtypeStruct((2 * SPAN, TILE, FAR_PARTS[0]), rows.dtype),
        in_specs=[pl.BlockSpec(memory_space=pl.ANY)],
        out_specs=pl.BlockSpec(memory_space=pltpu.VMEM),
        scratch_shapes=[pltpu.SemaphoreType.DMA((2 * PIECES,))],
        compiler_params=pltpu.CompilerParams(vmem_limit_bytes=52 * 2**20),
        cost_estimate=pl.CostEstimate(flops=0, bytes_accessed=1_600_000, transcendentals=0),
        name="cut",
    )(rows)


def section_specs(section, *arrays):
    def spec(shape):
        return pl.BlockSpec((1, *shape[1:]), lambda i: (section,) + (0,) * (len(shape) - 1))

    return [spec(array.shape) for array in arrays]


def prepare_kernel(*refs):
    low, high = place_bits()
    sections, rows = (refs[0:3], refs[3:6]), refs[6]
    far, *near, energy, near_data, last_data, image, sems = refs[7:]
    piece = image.shape[1] // PIECES
    loads = []
    for k in range(PIECES):
        some = pl.ds(k * piece, piece)
        loads.append(pltpu.make_async_copy(rows.at[:, some], image.at[:, some], sems.at[k]))
        loads[-1].start()
    for data, bit, section in zip((near_data, last_data), (low, high), sections):
        encode(data, bit, *(array.at[0] for array in section))
    width, each = far.shape[-1], DATA_TILES // 2
    for i in range(2):
        for k in range(each):
            far[2 * SPAN + 1 + i * each + k] = near_data[i, :, k * width : (k + 1) * width]

    def add(i, total):
        block = image[:, pl.ds(i * 4, 4)].astype(jnp.float32)
        return total + jnp.sum(block * block, axis=(0, 1))

    total = jnp.zeros(image.shape[2:], jnp.float32)
    for k in range(PIECES):
        loads[k].wait()
        total = lax.fori_loop(k * piece // 4, (k + 1) * piece // 4, add, total)
    energy[...] = jnp.broadcast_to(jnp.sum(total, keepdims=True), energy.shape)
    for half in range(2):
        place = slice(half * SPAN, (half + 1) * SPAN)
        far[place] = image[half, pl.ds(low * STEP, SPAN), :, FAR_PARTS[0] :]
        at = 0
        for part in near:
            width = part.shape[-1]
            part[place] = image[half, pl.ds((1 - low) * STEP, SPAN), :, at : at + width]
            at += width


def prepare(rows, section):
    bins = rows.shape[-1]
    sizes = [(2 * SPAN + 1 + DATA_TILES, FAR_PARTS[1])] + [(2 * SPAN + (i == 0), w) for i, w in enumerate(NEAR_PARTS)]
    shapes = [jax.ShapeDtypeStruct((tiles, TILE, w), rows.dtype) for tiles, w in sizes]
    shapes.append(jax.ShapeDtypeStruct((1, LANES), jnp.float32))
    shapes += [jax.ShapeDtypeStruct((2, TILE, bins), rows.dtype)] * 2
    return pl.pallas_call(
        prepare_kernel,
        grid=(1,),
        out_shape=shapes,
        in_specs=[*section_specs(0, *section), *section_specs(1, *section), pl.BlockSpec(memory_space=pl.ANY)],
        out_specs=[pl.BlockSpec(memory_space=pltpu.VMEM)] * len(shapes),
        scratch_shapes=[pltpu.VMEM(rows.shape, rows.dtype), pltpu.SemaphoreType.DMA((PIECES,))],
        compiler_params=pltpu.CompilerParams(vmem_limit_bytes=52 * 2**20),
        cost_estimate=pl.CostEstimate(flops=4 * SPAN * TILE * bins, bytes_accessed=4_000_000, transcendentals=0),
        name="prepare",
    )(*section, *section, rows)


def seal_kernel(far, near, energy, far_result, near_result, tail, sems):
    row = lax.broadcasted_iota(jnp.int32, (TILE, LANES), 0)
    value = jnp.zeros((TILE, LANES), jnp.float32)
    for i, term in enumerate(terms_of(energy[...])):
        value = jnp.where(row == i, term, value)
    tail[0] = value.astype(jnp.bfloat16)
    copies = [
        pltpu.make_async_copy(tail, result.at[pl.ds(2 * SPAN, 1), :, 0:LANES], sems.at[i])
        for i, result in enumerate((far_result, near_result))
    ]
    for copy in copies:
        copy.start()
    for copy in copies:
        copy.wait()


def seal(far, near, energy):
    anywhere = pl.BlockSpec(memory_space=pl.ANY)
    return pl.pallas_call(
        seal_kernel,
        out_shape=[jax.ShapeDtypeStruct(part.shape, part.dtype) for part in (far, near)],
        in_specs=[anywhere, anywhere, pl.BlockSpec(memory_space=pltpu.VMEM)],
        out_specs=[anywhere, anywhere],
        scratch_shapes=[pltpu.VMEM((1, TILE, LANES), far.dtype), pltpu.SemaphoreType.DMA((2,))],
        input_output_aliases={0: 0, 1: 1},
        compiler_params=pltpu.CompilerParams(vmem_limit_bytes=4 * 2**20),
        cost_estimate=pl.CostEstimate(flops=10_000, bytes_accessed=20_000, transcendentals=0),
        name="seal",
    )(far, near, energy)


def build_table(target, columns, first_row, row_tiles, group):
    rows = group * TILE
    lane = lax.broadcasted_iota(jnp.int32, (rows, LANES), 1)

    def step(i, carry):
        block = columns[pl.ds(pl.multiple_of(first_row + i * rows, TILE), rows), :]
        place = pl.ds(pl.multiple_of(i * rows, TILE), rows)

        def spread(column):
            return jnp.broadcast_to(block[:, column : column + 1], (rows, LANES))

        rest = jnp.zeros((rows, LANES), jnp.float32)
        for child in range(2):
            start = spread(2 * TAPS + child).astype(jnp.int32)
            taps = [spread(child * TAPS + t) for t in range(TAPS)]

            def entries(source, part):
                hit = source - start
                for t in range(TAPS):
                    part = jnp.where(hit == t, taps[t], part)
                return part

            for part in range(BULK // LANES):
                at = child * BULK + part * LANES
                target[place, at : at + LANES] = entries(lane + part * LANES, jnp.zeros((rows, LANES), jnp.float32))
            inside = (lane >= child * TILE) & (lane < (child + 1) * TILE)
            rest = entries(jnp.where(inside, lane + (BULK - child * TILE), -TAPS), rest)
        target[place, 2 * BULK : 2 * BAND] = rest[:, : 2 * TILE]
        return carry

    lax.fori_loop(0, row_tiles // group, step, 0)


def table_kernel(data, table, turn, columns):
    beams = columns.shape[0]
    taps, rest = decode(data)
    starts = jnp.concatenate([rest[:1, :beams], rest[:1, beams:], jnp.zeros((TILE - 2, beams), jnp.float32)])
    fill = jnp.zeros((LANES - 2 * TAPS - TILE, beams), jnp.float32)
    columns[...] = jnp.transpose(jnp.concatenate([taps[:, :beams], taps[:, beams:], starts, fill]))
    for child in range(2):
        at = 1 + child * TERMS
        phase = rest[at : at + 1] + rest[at + 1 : at + 2] + rest[at + 2 : at + 3]
        turn[2 * child : 2 * child + 1, :] = jnp.cos(phase)
        turn[2 * child + 1 : 2 * child + 2, :] = jnp.sin(phase)
    first_row = place_bits()[1] * (STEP * TILE) if table.shape[0] == BAND else 0
    row_tiles = table.shape[0] // TILE
    build_table(table, columns, first_row, row_tiles, 3 if row_tiles % 3 == 0 else 4)


def make_table(rows, data, beams):
    whole = pl.BlockSpec(memory_space=pltpu.VMEM)
    table, turn = pl.pallas_call(
        table_kernel,
        out_shape=[jax.ShapeDtypeStruct(s, jnp.float32) for s in ((rows, 2 * BAND), (4, 2 * beams))],
        in_specs=[whole],
        out_specs=[whole] * 2,
        scratch_shapes=[pltpu.VMEM((beams, LANES), jnp.float32)],
        compiler_params=pltpu.CompilerParams(vmem_limit_bytes=8 * 2**20),
        cost_estimate=pl.CostEstimate(flops=rows * 12_000, bytes_accessed=rows * 4096, transcendentals=8192),
        name="table",
    )(data)
    return table.astype(jnp.bfloat16), turn


def turned(real, imag, cosine, sine):
    return cosine * real - sine * imag, sine * real + cosine * imag


def joined(left, right):
    both = []
    for a, b in zip(left, right):
        both.append(jnp.concatenate([a[:BULK], b[:BULK], a[BULK:], b[BULK:]]).astype(jnp.bfloat16))
    return jnp.concatenate(both, axis=1)


def first_merges(images, tables, turns, gains):
    width = images[1].shape[-1]

    def child(source, turn, row, gain):
        real, imag = (
            source[half * SPAN : (half + 1) * SPAN].astype(jnp.float32).reshape(BAND, width) for half in range(2)
        )
        scale = jnp.concatenate([gain] * (width // LANES), axis=1)
        return turned(real, imag, scale * turn[row : row + 1, :], scale * turn[row + 1 : row + 2, :])

    def merge(left, right, table):
        merged = jnp.dot(table[...], joined(left, right), preferred_element_type=jnp.float32)
        return merged[:, :width], merged[:, width:]

    own, one, two, three = images
    near_turn, far_turn, last_turn = turns
    near = merge(child(own, near_turn, 0, gains[0:1]), child(one, near_turn, 2, gains[1:2]), tables[0])
    near = turned(*near, last_turn[0:1, :], last_turn[1:2, :])
    far = merge(child(two, far_turn, 0, gains[2:3]), child(three, far_turn, 2, gains[3:4]), tables[1])
    far = turned(*far, last_turn[2:3, :], last_turn[3:4, :])
    return joined(near, far)


def merge_kernel(cells, *refs):
    images, tables, turns, energies = refs[0:4], refs[4:7], refs[7:10], refs[10:14]
    result, gains = refs[14:16]

    def unsealed(tail):
        terms = tail[0].astype(jnp.float32)
        return terms[0:1] + terms[1:2] + terms[2:3]

    energy = jnp.concatenate([energies[0][...]] + [unsealed(tail) for tail in energies[1:]])
    gains[...] = lax.rsqrt(energy / cells + 1e-06)
    both = first_merges(images, tables, turns, gains[...])
    merged = jnp.dot(tables[2][...], both, preferred_element_type=jnp.float32)
    width = result.shape[-1]
    result[0, 0] = merged[:, :width].astype(jnp.bfloat16)
    result[0, 1] = merged[:, width:].astype(jnp.bfloat16)


def merge_cost(width, beams):
    flops = 8 * width * BAND * (2 * BAND + beams)
    return pl.CostEstimate(flops=flops, bytes_accessed=8192 * width, transcendentals=0)


def merge_first(images, tables, turns, energy, tails, cells, shape):
    width = images[1].shape[-1]
    beams = shape[2]
    in_specs = [pl.BlockSpec((image.shape[0], TILE, BLOCK), lambda i: (0, 0, i)) for image in images]
    in_specs += [pl.BlockSpec(t.shape, lambda i: (0, 0)) for t in tables]
    in_specs += [pl.BlockSpec((t.shape[0], BLOCK), lambda i: (0, i)) for t in turns]
    in_specs += [pl.BlockSpec((1, LANES), lambda i: (0, 0))]
    in_specs += [pl.BlockSpec((1, TILE, LANES), lambda i: (2 * SPAN, 0, 0)) for tail in tails]
    return pl.pallas_call(
        functools.partial(merge_kernel, cells),
        grid=(width // BLOCK,),
        out_shape=[jax.ShapeDtypeStruct(shape, jnp.bfloat16), jax.ShapeDtypeStruct((GROUP, LANES), jnp.float32)],
        in_specs=in_specs,
        out_specs=[
            pl.BlockSpec((1, 2, beams, BLOCK), lambda i: (0, 0, 0, i)),
            pl.BlockSpec((GROUP, LANES), lambda i: (0, 0)),
        ],
        compiler_params=pltpu.CompilerParams(vmem_limit_bytes=16 * 2**20),
        cost_estimate=merge_cost(width, beams),
        name="merge",
    )(*images, *tables, *turns, energy, *tails)


def finish_kernel(at, skip, *refs):
    images, tables, turns, gains = refs[0:4], refs[4:7], refs[7:10], refs[10]
    result, buffer, sems = refs[12:15]
    width = buffer.shape[-1]
    bins = slice(at, at + width)
    own, one, two, three = images
    cut = [own[:, :, skip : skip + width], one[...], two[:, :, skip : skip + width], three[...]]
    both = first_merges(cut, tables, [turn[:, bins] for turn in turns], gains[...])
    copies = []
    for k, row in enumerate(range(0, buffer.shape[1], OUT_ROWS)):
        rows = slice(row, row + OUT_ROWS)
        merged = jnp.dot(tables[2][rows, :], both, preferred_element_type=jnp.float32)
        for half in range(2):
            buffer[half, rows] = merged[:, half * width : (half + 1) * width].astype(jnp.bfloat16)
        copies.append(pltpu.make_async_copy(buffer.at[:, rows], result.at[0, :, rows, bins], sems.at[k]))
        copies[-1].start()
    for copy in copies:
        copy.wait()


def finish(prior, at, images, tables, turns, gains):
    width = images[1].shape[-1]
    beams = prior.shape[2]
    operands = [*images, *tables, *turns, gains]
    return pl.pallas_call(
        functools.partial(finish_kernel, at, at % FAR_PARTS[0]),
        out_shape=jax.ShapeDtypeStruct(prior.shape, prior.dtype),
        in_specs=[pl.BlockSpec(memory_space=pltpu.VMEM)] * len(operands) + [pl.BlockSpec(memory_space=pl.ANY)],
        out_specs=pl.BlockSpec(memory_space=pl.ANY),
        scratch_shapes=[pltpu.VMEM((2, beams, width), prior.dtype), pltpu.SemaphoreType.DMA((beams // OUT_ROWS,))],
        input_output_aliases={len(operands): 0},
        compiler_params=pltpu.CompilerParams(vmem_limit_bytes=16 * 2**20),
        cost_estimate=merge_cost(width, beams),
        name="finish",
    )(*operands, prior)


def shards(polar, autofocus, offsets, weights):
    beams, bins = polar.shape[2], polar.shape[3]
    cells = 2 * beams * lax.axis_size("sec") * bins // 2
    rows = polar.reshape(2, beams // TILE, TILE, bins)

    first = cut(rows)
    far = [partner(first, 2)]
    rows, first = lax.optimization_barrier((rows, first))
    second, *near, energy, near_data, last_data = prepare(rows, (weights, offsets, autofocus))
    energy = lax.psum(energy, "sec")
    second, near[0] = seal(second, near[0], energy)
    far.append(partner(second, 2))
    near_table, near_turn = make_table(BAND, near_data, beams)
    last_table, last_turn = make_table(beams, last_data, beams)
    near[1], far[0], near_table, last_table = lax.optimization_barrier((near[1], far[0], near_table, last_table))
    one, three = ([partner(part, flip) for part in near] for flip in (1, 3))
    far_table, far_turn = make_table(BAND, far[1], beams)

    tables = [near_table, far_table, last_table]
    turns = [near_turn, far_turn, last_turn]
    images = [first, one[0], far[0], three[0]]
    merged, gains = merge_first(images, tables, turns, energy, [one[0], far[1], three[0]], cells, polar.shape)
    return finish(merged, NEAR_PARTS[0], [second, one[1], far[1], three[1]], tables, turns, gains)


def solution(mesh):
    ring = Mesh(mesh.devices.reshape(-1, GROUP, mesh.devices.shape[1]), ("rest", "x", "sec"))
    placed = (
        P(("rest", "x"), None, "sec", None),
        P(None, None, ("rest", "x"), None),
        P(None, None, ("rest", "x"), "sec"),
        P(None, None, ("rest", "x"), None, "sec"),
    )
    return jax.shard_map(
        shards, mesh=ring, in_specs=placed, out_specs=P(("rest", "x"), None, "sec", None), check_vma=False
    )
```

```python
import functools

import jax
import jax.numpy as jnp
from jax import lax
from jax.experimental import pallas as pl
from jax.experimental.pallas import tpu as pltpu
from jax.sharding import Mesh
from jax.sharding import PartitionSpec as P

GROUP = 4
TILE = 8
STEP = 31
SPAN = 33
BAND = SPAN * TILE
BULK = 256
TAPS = 8
LANES = 128
BLOCK = 256
OUT_ROWS = 256
FAR_PARTS = (768, 256)
NEAR_PARTS = (768, 256)
DATA_TILES = 8
PIECES = 4
TERMS = 3


def partner(value, flip):
    return lax.ppermute(value, "x", [(i, i ^ flip) for i in range(GROUP)])


def terms_of(value):
    terms = []
    for _ in range(TERMS):
        terms.append(value.astype(jnp.bfloat16).astype(jnp.float32))
        value = value - terms[-1]
    return terms


def place_bits():
    place = lax.axis_index("x")
    return place % 2, place // 2


def encode(tail, bit, weights, offsets, phases):
    beams = weights.shape[-1]
    own = bit == 0
    starts, angles = [], []
    for child in range(2):
        lanes = slice(child * beams, (child + 1) * beams)
        taps = jnp.where(own, weights[child, 0], weights[1 - child, 0])
        tail[0, :, lanes] = taps.astype(jnp.bfloat16)
        start = jnp.where(own, offsets[child], offsets[1 - child]) - bit * (STEP * TILE)
        starts.append(start.astype(jnp.float32))
        angles += terms_of(jnp.where(own, phases[child], phases[1 - child]))
    rows = [jnp.concatenate(starts, axis=1)] + angles
    rows.append(jnp.zeros((TILE - len(rows), 2 * beams), jnp.float32))
    tail[1] = jnp.concatenate(rows).astype(jnp.bfloat16)


def decode(data):
    if data.shape[0] == 2:
        return data[0].astype(jnp.float32), data[1].astype(jnp.float32)
    at, each = 2 * SPAN + 1, DATA_TILES // 2
    return [
        jnp.concatenate([data[at + i * each + k].astype(jnp.float32) for k in range(each)], axis=1) for i in range(2)
    ]


def cut_kernel(rows, result, sems):
    low, _ = place_bits()
    copies = []
    for half in range(2):
        for i in range(PIECES):
            at, end = SPAN * i // PIECES, SPAN * (i + 1) // PIECES
            source = rows.at[half, pl.ds(low * STEP + at, end - at), :, 0 : result.shape[-1]]
            target = result.at[pl.ds(half * SPAN + at, end - at)]
            copies.append(pltpu.make_async_copy(source, target, sems.at[len(copies)]))
            copies[-1].start()
    for copy in copies:
        copy.wait()


def cut(rows):
    return pl.pallas_call(
        cut_kernel,
        out_shape=jax.ShapeDtypeStruct((2 * SPAN, TILE, FAR_PARTS[0]), rows.dtype),
        in_specs=[pl.BlockSpec(memory_space=pl.ANY)],
        out_specs=pl.BlockSpec(memory_space=pltpu.VMEM),
        scratch_shapes=[pltpu.SemaphoreType.DMA((2 * PIECES,))],
        compiler_params=pltpu.CompilerParams(vmem_limit_bytes=52 * 2**20),
        cost_estimate=pl.CostEstimate(flops=0, bytes_accessed=1_600_000, transcendentals=0),
        name="cut",
    )(rows)


def section_specs(section, *arrays):
    def spec(shape):
        return pl.BlockSpec((1, *shape[1:]), lambda i: (section,) + (0,) * (len(shape) - 1))

    return [spec(array.shape) for array in arrays]


def prepare_kernel(*refs):
    low, high = place_bits()
    sections, rows = (refs[0:3], refs[3:6]), refs[6]
    far, *near, energy, near_data, last_data, image, sems = refs[7:]
    piece = image.shape[1] // PIECES
    loads = []
    for k in range(PIECES):
        some = pl.ds(k * piece, piece)
        loads.append(pltpu.make_async_copy(rows.at[:, some], image.at[:, some], sems.at[k]))
        loads[-1].start()
    for data, bit, section in zip((near_data, last_data), (low, high), sections):
        encode(data, bit, *(array.at[0] for array in section))
    width, each = far.shape[-1], DATA_TILES // 2
    for i in range(2):
        for k in range(each):
            far[2 * SPAN + 1 + i * each + k] = near_data[i, :, k * width : (k + 1) * width]

    def add(i, total):
        block = image[:, pl.ds(i * 4, 4)].astype(jnp.float32)
        return total + jnp.sum(block * block, axis=(0, 1))

    total = jnp.zeros(image.shape[2:], jnp.float32)
    for k in range(PIECES):
        loads[k].wait()
        total = lax.fori_loop(k * piece // 4, (k + 1) * piece // 4, add, total)
    energy[...] = jnp.broadcast_to(jnp.sum(total, keepdims=True), energy.shape)
    for half in range(2):
        place = slice(half * SPAN, (half + 1) * SPAN)
        far[place] = image[half, pl.ds(low * STEP, SPAN), :, FAR_PARTS[0] :]
        at = 0
        for part in near:
            width = part.shape[-1]
            part[place] = image[half, pl.ds((1 - low) * STEP, SPAN), :, at : at + width]
            at += width


def prepare(rows, section):
    bins = rows.shape[-1]
    sizes = [(2 * SPAN + 1 + DATA_TILES, FAR_PARTS[1])] + [(2 * SPAN + (i == 0), w) for i, w in enumerate(NEAR_PARTS)]
    shapes = [jax.ShapeDtypeStruct((tiles, TILE, w), rows.dtype) for tiles, w in sizes]
    shapes.append(jax.ShapeDtypeStruct((1, LANES), jnp.float32))
    shapes += [jax.ShapeDtypeStruct((2, TILE, bins), rows.dtype)] * 2
    return pl.pallas_call(
        prepare_kernel,
        grid=(1,),
        out_shape=shapes,
        in_specs=[*section_specs(0, *section), *section_specs(1, *section), pl.BlockSpec(memory_space=pl.ANY)],
        out_specs=[pl.BlockSpec(memory_space=pltpu.VMEM)] * len(shapes),
        scratch_shapes=[pltpu.VMEM(rows.shape, rows.dtype), pltpu.SemaphoreType.DMA((PIECES,))],
        compiler_params=pltpu.CompilerParams(vmem_limit_bytes=52 * 2**20),
        cost_estimate=pl.CostEstimate(flops=4 * SPAN * TILE * bins, bytes_accessed=4_000_000, transcendentals=0),
        name="prepare",
    )(*section, *section, rows)


def seal_kernel(far, near, energy, far_result, near_result, tail, sems):
    row = lax.broadcasted_iota(jnp.int32, (TILE, LANES), 0)
    value = jnp.zeros((TILE, LANES), jnp.float32)
    for i, term in enumerate(terms_of(energy[...])):
        value = jnp.where(row == i, term, value)
    tail[0] = value.astype(jnp.bfloat16)
    copies = [
        pltpu.make_async_copy(tail, result.at[pl.ds(2 * SPAN, 1), :, 0:LANES], sems.at[i])
        for i, result in enumerate((far_result, near_result))
    ]
    for copy in copies:
        copy.start()
    for copy in copies:
        copy.wait()


def seal(far, near, energy):
    anywhere = pl.BlockSpec(memory_space=pl.ANY)
    return pl.pallas_call(
        seal_kernel,
        out_shape=[jax.ShapeDtypeStruct(part.shape, part.dtype) for part in (far, near)],
        in_specs=[anywhere, anywhere, pl.BlockSpec(memory_space=pltpu.VMEM)],
        out_specs=[anywhere, anywhere],
        scratch_shapes=[pltpu.VMEM((1, TILE, LANES), far.dtype), pltpu.SemaphoreType.DMA((2,))],
        input_output_aliases={0: 0, 1: 1},
        compiler_params=pltpu.CompilerParams(vmem_limit_bytes=4 * 2**20),
        cost_estimate=pl.CostEstimate(flops=10_000, bytes_accessed=20_000, transcendentals=0),
        name="seal",
    )(far, near, energy)


def build_table(target, columns, first_row, row_tiles, group):
    rows = group * TILE
    lane = lax.broadcasted_iota(jnp.int32, (rows, LANES), 1)

    def step(i, carry):
        block = columns[pl.ds(pl.multiple_of(first_row + i * rows, TILE), rows), :]
        place = pl.ds(pl.multiple_of(i * rows, TILE), rows)

        def spread(column):
            return jnp.broadcast_to(block[:, column : column + 1], (rows, LANES))

        rest = jnp.zeros((rows, LANES), jnp.float32)
        for child in range(2):
            start = spread(2 * TAPS + child).astype(jnp.int32)
            taps = [spread(child * TAPS + t) for t in range(TAPS)]

            def entries(source, part):
                hit = source - start
                for t in range(TAPS):
                    part = jnp.where(hit == t, taps[t], part)
                return part

            for part in range(BULK // LANES):
                at = child * BULK + part * LANES
                target[place, at : at + LANES] = entries(lane + part * LANES, jnp.zeros((rows, LANES), jnp.float32))
            inside = (lane >= child * TILE) & (lane < (child + 1) * TILE)
            rest = entries(jnp.where(inside, lane + (BULK - child * TILE), -TAPS), rest)
        target[place, 2 * BULK : 2 * BAND] = rest[:, : 2 * TILE]
        return carry

    lax.fori_loop(0, row_tiles // group, step, 0)


def table_kernel(data, table, turn, columns):
    beams = columns.shape[0]
    taps, rest = decode(data)
    starts = jnp.concatenate([rest[:1, :beams], rest[:1, beams:], jnp.zeros((TILE - 2, beams), jnp.float32)])
    fill = jnp.zeros((LANES - 2 * TAPS - TILE, beams), jnp.float32)
    columns[...] = jnp.transpose(jnp.concatenate([taps[:, :beams], taps[:, beams:], starts, fill]))
    for child in range(2):
        at = 1 + child * TERMS
        phase = rest[at : at + 1] + rest[at + 1 : at + 2] + rest[at + 2 : at + 3]
        turn[2 * child : 2 * child + 1, :] = jnp.cos(phase)
        turn[2 * child + 1 : 2 * child + 2, :] = jnp.sin(phase)
    first_row = place_bits()[1] * (STEP * TILE) if table.shape[0] == BAND else 0
    row_tiles = table.shape[0] // TILE
    build_table(table, columns, first_row, row_tiles, 3 if row_tiles % 3 == 0 else 4)


def make_table(rows, data, beams):
    whole = pl.BlockSpec(memory_space=pltpu.VMEM)
    table, turn = pl.pallas_call(
        table_kernel,
        out_shape=[jax.ShapeDtypeStruct(s, jnp.float32) for s in ((rows, 2 * BAND), (4, 2 * beams))],
        in_specs=[whole],
        out_specs=[whole] * 2,
        scratch_shapes=[pltpu.VMEM((beams, LANES), jnp.float32)],
        compiler_params=pltpu.CompilerParams(vmem_limit_bytes=8 * 2**20),
        cost_estimate=pl.CostEstimate(flops=rows * 12_000, bytes_accessed=rows * 4096, transcendentals=8192),
        name="table",
    )(data)
    return table.astype(jnp.bfloat16), turn


def turned(real, imag, cosine, sine):
    return cosine * real - sine * imag, sine * real + cosine * imag


def joined(left, right):
    both = []
    for a, b in zip(left, right):
        both.append(jnp.concatenate([a[:BULK], b[:BULK], a[BULK:], b[BULK:]]).astype(jnp.bfloat16))
    return jnp.concatenate(both, axis=1)


def first_merge(images, table, turn, last_turn, gains):
    width = images[1].shape[-1]

    def child(source, row, gain):
        real, imag = (
            source[half * SPAN : (half + 1) * SPAN].astype(jnp.float32).reshape(BAND, width) for half in range(2)
        )
        scale = jnp.concatenate([gain] * (width // LANES), axis=1)
        return turned(real, imag, scale * turn[row : row + 1, :], scale * turn[row + 1 : row + 2, :])

    both = joined(child(images[0], 0, gains[0:1]), child(images[1], 2, gains[1:2]))
    merged = jnp.dot(table[...], both, preferred_element_type=jnp.float32)
    return turned(merged[:, :width], merged[:, width:], last_turn[0:1, :], last_turn[1:2, :])


def unsealed(tail):
    terms = tail[0].astype(jnp.float32)
    return terms[0:1] + terms[1:2] + terms[2:3]


def gains_of(energies, cells):
    energy = jnp.concatenate([energies[0][...]] + [unsealed(tail) for tail in energies[1:]])
    return lax.rsqrt(energy / cells + 1e-06)


def near_kernel(cells, own, one, table, turn, last_turn, energy, one_tail, result):
    gains = gains_of([energy, one_tail], cells)
    real, imag = first_merge((own, one), table, turn, last_turn[0:2, :], gains)
    result[0] = real
    result[1] = imag


def far_kernel(cells, near, two, three, far_table, last_table, turn, last_turn, *refs):
    *energies, result, gains = refs
    gains[...] = gains_of(energies, cells)
    far = first_merge((two, three), far_table, turn, last_turn[2:4, :], gains[2:4])
    both = joined((near[0], near[1]), far)
    merged = jnp.dot(last_table[...], both, preferred_element_type=jnp.float32)
    width = result.shape[-1]
    result[0, 0] = merged[:, :width].astype(jnp.bfloat16)
    result[0, 1] = merged[:, width:].astype(jnp.bfloat16)


def merge_cost(width, rows):
    flops = 8 * width * BAND * rows
    return pl.CostEstimate(flops=flops, bytes_accessed=6000 * width, transcendentals=0)


def image_spec(image):
    return pl.BlockSpec((image.shape[0], TILE, BLOCK), lambda i: (0, 0, i))


def turn_spec(turn):
    return pl.BlockSpec((turn.shape[0], BLOCK), lambda i: (0, i))


def whole_spec(array):
    return pl.BlockSpec(array.shape, lambda i: (0,) * len(array.shape))


def tail_spec(tail):
    return pl.BlockSpec((1, TILE, LANES), lambda i: (2 * SPAN, 0, 0))


def merge_near(own, one, table, turn, last_turn, energy, cells):
    width = one.shape[-1]
    return pl.pallas_call(
        functools.partial(near_kernel, cells),
        grid=(width // BLOCK,),
        out_shape=jax.ShapeDtypeStruct((2, BAND, width), jnp.float32),
        in_specs=[
            image_spec(own),
            image_spec(one),
            whole_spec(table),
            turn_spec(turn),
            turn_spec(last_turn),
            whole_spec(energy),
            tail_spec(one),
        ],
        out_specs=pl.BlockSpec((2, BAND, BLOCK), lambda i: (0, 0, i)),
        compiler_params=pltpu.CompilerParams(vmem_limit_bytes=12 * 2**20),
        cost_estimate=merge_cost(width, BAND),
        name="near",
    )(own, one, table, turn, last_turn, energy, one)


def merge_far(near, two, three, tables, turns, energy, tails, cells, shape):
    width = three.shape[-1]
    beams = shape[2]
    return pl.pallas_call(
        functools.partial(far_kernel, cells),
        grid=(width // BLOCK,),
        out_shape=[jax.ShapeDtypeStruct(shape, jnp.bfloat16), jax.ShapeDtypeStruct((GROUP, LANES), jnp.float32)],
        in_specs=[
            pl.BlockSpec((2, BAND, BLOCK), lambda i: (0, 0, i)),
            image_spec(two),
            image_spec(three),
            *[whole_spec(table) for table in tables],
            *[turn_spec(turn) for turn in turns],
            whole_spec(energy),
            *[tail_spec(tail) for tail in tails],
        ],
        out_specs=[
            pl.BlockSpec((1, 2, beams, BLOCK), lambda i: (0, 0, 0, i)),
            pl.BlockSpec((GROUP, LANES), lambda i: (0, 0)),
        ],
        compiler_params=pltpu.CompilerParams(vmem_limit_bytes=16 * 2**20),
        cost_estimate=merge_cost(width, BAND + beams),
        name="merge",
    )(near, two, three, *tables, *turns, energy, *tails)


def finish_kernel(at, skip, *refs):
    images, tables, turns, gains = refs[0:4], refs[4:7], refs[7:10], refs[10]
    result, buffer, sems = refs[12:15]
    width = buffer.shape[-1]
    bins = slice(at, at + width)
    own, one, two, three = images
    near_turn, far_turn, last_turn = (turn[:, bins] for turn in turns)
    near = first_merge((own[:, :, skip : skip + width], one), tables[0], near_turn, last_turn[0:2], gains[0:2])
    far = first_merge((two[:, :, skip : skip + width], three), tables[1], far_turn, last_turn[2:4], gains[2:4])
    both = joined(near, far)
    copies = []
    for k, row in enumerate(range(0, buffer.shape[1], OUT_ROWS)):
        rows = slice(row, row + OUT_ROWS)
        merged = jnp.dot(tables[2][rows, :], both, preferred_element_type=jnp.float32)
        for half in range(2):
            buffer[half, rows] = merged[:, half * width : (half + 1) * width].astype(jnp.bfloat16)
        copies.append(pltpu.make_async_copy(buffer.at[:, rows], result.at[0, :, rows, bins], sems.at[k]))
        copies[-1].start()
    for copy in copies:
        copy.wait()


def finish(prior, at, images, tables, turns, gains):
    width = images[1].shape[-1]
    beams = prior.shape[2]
    operands = [*images, *tables, *turns, gains]
    return pl.pallas_call(
        functools.partial(finish_kernel, at, at % FAR_PARTS[0]),
        out_shape=jax.ShapeDtypeStruct(prior.shape, prior.dtype),
        in_specs=[pl.BlockSpec(memory_space=pltpu.VMEM)] * len(operands) + [pl.BlockSpec(memory_space=pl.ANY)],
        out_specs=pl.BlockSpec(memory_space=pl.ANY),
        scratch_shapes=[pltpu.VMEM((2, beams, width), prior.dtype), pltpu.SemaphoreType.DMA((beams // OUT_ROWS,))],
        input_output_aliases={len(operands): 0},
        compiler_params=pltpu.CompilerParams(vmem_limit_bytes=16 * 2**20),
        cost_estimate=merge_cost(width, 2 * BAND + beams),
        name="finish",
    )(*operands, prior)


def shards(polar, autofocus, offsets, weights):
    beams, bins = polar.shape[2], polar.shape[3]
    cells = 2 * beams * lax.axis_size("sec") * bins // 2
    rows = polar.reshape(2, beams // TILE, TILE, bins)

    first = cut(rows)
    far = [partner(first, 2)]
    rows, first = lax.optimization_barrier((rows, first))
    second, *near, energy, near_data, last_data = prepare(rows, (weights, offsets, autofocus))
    energy = lax.psum(energy, "sec")
    second, near[0] = seal(second, near[0], energy)
    far.append(partner(second, 2))
    near_table, near_turn = make_table(BAND, near_data, beams)
    last_table, last_turn = make_table(beams, last_data, beams)
    near[1], far[0], near_table, last_table = lax.optimization_barrier((near[1], far[0], near_table, last_table))
    one, three = ([partner(part, flip) for part in near] for flip in (1, 3))
    merged_near = merge_near(first, one[0], near_table, near_turn, last_turn, energy, cells)
    far[1], merged_near = lax.optimization_barrier((far[1], merged_near))
    far_table, far_turn = make_table(BAND, far[1], beams)
    tails = [one[0], far[1], three[0]]
    tables, turns = [far_table, last_table], [far_turn, last_turn]
    merged, gains = merge_far(merged_near, far[0], three[0], tables, turns, energy, tails, cells, polar.shape)
    tables, turns = [near_table, far_table, last_table], [near_turn, far_turn, last_turn]
    return finish(merged, NEAR_PARTS[0], [second, one[1], far[1], three[1]], tables, turns, gains)


def solution(mesh):
    ring = Mesh(mesh.devices.reshape(-1, GROUP, mesh.devices.shape[1]), ("rest", "x", "sec"))
    placed = (
        P(("rest", "x"), None, "sec", None),
        P(None, None, ("rest", "x"), None),
        P(None, None, ("rest", "x"), "sec"),
        P(None, None, ("rest", "x"), None, "sec"),
    )
    return jax.shard_map(
        shards, mesh=ring, in_specs=placed, out_specs=P(("rest", "x"), None, "sec", None), check_vma=False
    )
```

```python
import functools

import jax
import jax.numpy as jnp
from jax import lax
from jax.experimental import pallas as pl
from jax.experimental.pallas import tpu as pltpu
from jax.sharding import Mesh
from jax.sharding import PartitionSpec as P

GROUP = 4
TILE = 8
STEP = 31
SPAN = 33
BAND = SPAN * TILE
BULK = 256
TAPS = 8
LANES = 128
BLOCK = 384
OUT_ROWS = 256
FAR_PARTS = (640, 384)
NEAR_PARTS = (384, 384, 256)
DATA_TILES = 6
PIECES = 4
TERMS = 3


def partner(value, flip):
    return lax.ppermute(value, "x", [(i, i ^ flip) for i in range(GROUP)])


def terms_of(value):
    terms = []
    for _ in range(TERMS):
        terms.append(value.astype(jnp.bfloat16).astype(jnp.float32))
        value = value - terms[-1]
    return terms


def place_bits():
    place = lax.axis_index("x")
    return place % 2, place // 2


def encode(tail, bit, weights, offsets, phases):
    beams = weights.shape[-1]
    own = bit == 0
    starts, angles = [], []
    for child in range(2):
        lanes = slice(child * beams, (child + 1) * beams)
        taps = jnp.where(own, weights[child, 0], weights[1 - child, 0])
        tail[0, :, lanes] = taps.astype(jnp.bfloat16)
        start = jnp.where(own, offsets[child], offsets[1 - child]) - bit * (STEP * TILE)
        starts.append(start.astype(jnp.float32))
        angles += terms_of(jnp.where(own, phases[child], phases[1 - child]))
    rows = [jnp.concatenate(starts, axis=1)] + angles
    rows.append(jnp.zeros((TILE - len(rows), 2 * beams), jnp.float32))
    tail[1] = jnp.concatenate(rows).astype(jnp.bfloat16)


def decode(data, lanes):
    if data.shape[0] == 2:
        return data[0].astype(jnp.float32), data[1].astype(jnp.float32)
    at, each = 2 * SPAN + 1, DATA_TILES // 2
    return [
        jnp.concatenate([data[at + i * each + k].astype(jnp.float32) for k in range(each)], axis=1)[:, :lanes]
        for i in range(2)
    ]


def cut_kernel(rows, result, sems):
    low, _ = place_bits()
    copies = []
    for half in range(2):
        for i in range(PIECES):
            at, end = SPAN * i // PIECES, SPAN * (i + 1) // PIECES
            source = rows.at[half, pl.ds(low * STEP + at, end - at), :, 0 : result.shape[-1]]
            target = result.at[pl.ds(half * SPAN + at, end - at)]
            copies.append(pltpu.make_async_copy(source, target, sems.at[len(copies)]))
            copies[-1].start()
    for copy in copies:
        copy.wait()


def cut(rows):
    return pl.pallas_call(
        cut_kernel,
        out_shape=jax.ShapeDtypeStruct((2 * SPAN, TILE, FAR_PARTS[0]), rows.dtype),
        in_specs=[pl.BlockSpec(memory_space=pl.ANY)],
        out_specs=pl.BlockSpec(memory_space=pltpu.VMEM),
        scratch_shapes=[pltpu.SemaphoreType.DMA((2 * PIECES,))],
        compiler_params=pltpu.CompilerParams(vmem_limit_bytes=52 * 2**20),
        cost_estimate=pl.CostEstimate(flops=0, bytes_accessed=1_600_000, transcendentals=0),
        name="cut",
    )(rows)


def section_specs(section, *arrays):
    def spec(shape):
        return pl.BlockSpec((1, *shape[1:]), lambda i: (section,) + (0,) * (len(shape) - 1))

    return [spec(array.shape) for array in arrays]


def prepare_kernel(*refs):
    low, high = place_bits()
    sections, rows = (refs[0:3], refs[3:6]), refs[6]
    far, *near, energy, near_data, last_data, image, sems = refs[7:]
    piece = image.shape[1] // PIECES
    loads = []
    for k in range(PIECES):
        some = pl.ds(k * piece, piece)
        loads.append(pltpu.make_async_copy(rows.at[:, some], image.at[:, some], sems.at[k]))
        loads[-1].start()
    for data, bit, section in zip((near_data, last_data), (low, high), sections):
        encode(data, bit, *(array.at[0] for array in section))
    width, each = far.shape[-1], DATA_TILES // 2
    for i in range(2):
        for k in range(each):
            some = near_data[i, :, k * width : (k + 1) * width]
            far[2 * SPAN + 1 + i * each + k, :, 0 : some.shape[-1]] = some

    def add(i, total):
        block = image[:, pl.ds(i * 4, 4)].astype(jnp.float32)
        return total + jnp.sum(block * block, axis=(0, 1))

    total = jnp.zeros(image.shape[2:], jnp.float32)
    for k in range(PIECES):
        loads[k].wait()
        total = lax.fori_loop(k * piece // 4, (k + 1) * piece // 4, add, total)
    energy[...] = jnp.broadcast_to(jnp.sum(total, keepdims=True), energy.shape)
    for half in range(2):
        place = slice(half * SPAN, (half + 1) * SPAN)
        far[place] = image[half, pl.ds(low * STEP, SPAN), :, FAR_PARTS[0] :]
        at = 0
        for part in near:
            width = part.shape[-1]
            part[place] = image[half, pl.ds((1 - low) * STEP, SPAN), :, at : at + width]
            at += width


def prepare(rows, section):
    bins = rows.shape[-1]
    sizes = [(2 * SPAN + 1 + DATA_TILES, FAR_PARTS[1])] + [(2 * SPAN + (i == 0), w) for i, w in enumerate(NEAR_PARTS)]
    shapes = [jax.ShapeDtypeStruct((tiles, TILE, w), rows.dtype) for tiles, w in sizes]
    shapes.append(jax.ShapeDtypeStruct((1, LANES), jnp.float32))
    shapes += [jax.ShapeDtypeStruct((2, TILE, bins), rows.dtype)] * 2
    return pl.pallas_call(
        prepare_kernel,
        grid=(1,),
        out_shape=shapes,
        in_specs=[*section_specs(0, *section), *section_specs(1, *section), pl.BlockSpec(memory_space=pl.ANY)],
        out_specs=[pl.BlockSpec(memory_space=pltpu.VMEM)] * len(shapes),
        scratch_shapes=[pltpu.VMEM(rows.shape, rows.dtype), pltpu.SemaphoreType.DMA((PIECES,))],
        compiler_params=pltpu.CompilerParams(vmem_limit_bytes=52 * 2**20),
        cost_estimate=pl.CostEstimate(flops=4 * SPAN * TILE * bins, bytes_accessed=4_000_000, transcendentals=0),
        name="prepare",
    )(*section, *section, rows)


def seal_kernel(far, near, energy, far_result, near_result, tail, sems):
    row = lax.broadcasted_iota(jnp.int32, (TILE, LANES), 0)
    value = jnp.zeros((TILE, LANES), jnp.float32)
    for i, term in enumerate(terms_of(energy[...])):
        value = jnp.where(row == i, term, value)
    tail[0] = value.astype(jnp.bfloat16)
    copies = [
        pltpu.make_async_copy(tail, result.at[pl.ds(2 * SPAN, 1), :, 0:LANES], sems.at[i])
        for i, result in enumerate((far_result, near_result))
    ]
    for copy in copies:
        copy.start()
    for copy in copies:
        copy.wait()


def seal(far, near, energy):
    anywhere = pl.BlockSpec(memory_space=pl.ANY)
    return pl.pallas_call(
        seal_kernel,
        out_shape=[jax.ShapeDtypeStruct(part.shape, part.dtype) for part in (far, near)],
        in_specs=[anywhere, anywhere, pl.BlockSpec(memory_space=pltpu.VMEM)],
        out_specs=[anywhere, anywhere],
        scratch_shapes=[pltpu.VMEM((1, TILE, LANES), far.dtype), pltpu.SemaphoreType.DMA((2,))],
        input_output_aliases={0: 0, 1: 1},
        compiler_params=pltpu.CompilerParams(vmem_limit_bytes=4 * 2**20),
        cost_estimate=pl.CostEstimate(flops=10_000, bytes_accessed=20_000, transcendentals=0),
        name="seal",
    )(far, near, energy)


def build_table(target, columns, first_row, row_tiles, group):
    rows = group * TILE
    lane = lax.broadcasted_iota(jnp.int32, (rows, LANES), 1)

    def step(i, carry):
        block = columns[pl.ds(pl.multiple_of(first_row + i * rows, TILE), rows), :]
        place = pl.ds(pl.multiple_of(i * rows, TILE), rows)

        def spread(column):
            return jnp.broadcast_to(block[:, column : column + 1], (rows, LANES))

        rest = jnp.zeros((rows, LANES), jnp.float32)
        for child in range(2):
            start = spread(2 * TAPS + child).astype(jnp.int32)
            taps = [spread(child * TAPS + t) for t in range(TAPS)]

            def entries(source, part):
                hit = source - start
                for t in range(TAPS):
                    part = jnp.where(hit == t, taps[t], part)
                return part

            for part in range(BULK // LANES):
                at = child * BULK + part * LANES
                target[place, at : at + LANES] = entries(lane + part * LANES, jnp.zeros((rows, LANES), jnp.float32))
            inside = (lane >= child * TILE) & (lane < (child + 1) * TILE)
            rest = entries(jnp.where(inside, lane + (BULK - child * TILE), -TAPS), rest)
        target[place, 2 * BULK : 2 * BAND] = rest[:, : 2 * TILE]
        return carry

    lax.fori_loop(0, row_tiles // group, step, 0)


def table_kernel(data, table, turn, columns):
    beams = columns.shape[0]
    taps, rest = decode(data, 2 * beams)
    starts = jnp.concatenate([rest[:1, :beams], rest[:1, beams:], jnp.zeros((TILE - 2, beams), jnp.float32)])
    fill = jnp.zeros((LANES - 2 * TAPS - TILE, beams), jnp.float32)
    columns[...] = jnp.transpose(jnp.concatenate([taps[:, :beams], taps[:, beams:], starts, fill]))
    for child in range(2):
        at = 1 + child * TERMS
        phase = rest[at : at + 1] + rest[at + 1 : at + 2] + rest[at + 2 : at + 3]
        turn[2 * child : 2 * child + 1, :] = jnp.cos(phase)
        turn[2 * child + 1 : 2 * child + 2, :] = jnp.sin(phase)
    first_row = place_bits()[1] * (STEP * TILE) if table.shape[0] == BAND else 0
    row_tiles = table.shape[0] // TILE
    build_table(table, columns, first_row, row_tiles, 3 if row_tiles % 3 == 0 else 4)


def make_table(rows, data, beams):
    whole = pl.BlockSpec(memory_space=pltpu.VMEM)
    table, turn = pl.pallas_call(
        table_kernel,
        out_shape=[jax.ShapeDtypeStruct(s, jnp.float32) for s in ((rows, 2 * BAND), (4, 2 * beams))],
        in_specs=[whole],
        out_specs=[whole] * 2,
        scratch_shapes=[pltpu.VMEM((beams, LANES), jnp.float32)],
        compiler_params=pltpu.CompilerParams(vmem_limit_bytes=8 * 2**20),
        cost_estimate=pl.CostEstimate(flops=rows * 12_000, bytes_accessed=rows * 4096, transcendentals=8192),
        name="table",
    )(data)
    return table.astype(jnp.bfloat16), turn


def turned(real, imag, cosine, sine):
    return cosine * real - sine * imag, sine * real + cosine * imag


def joined(left, right):
    both = []
    for a, b in zip(left, right):
        both.append(jnp.concatenate([a[:BULK], b[:BULK], a[BULK:], b[BULK:]]).astype(jnp.bfloat16))
    return jnp.concatenate(both, axis=1)


def first_merges(images, tables, turns, gains):
    width = images[1].shape[-1]

    def child(source, turn, row, gain):
        real, imag = (
            source[half * SPAN : (half + 1) * SPAN].astype(jnp.float32).reshape(BAND, width) for half in range(2)
        )
        scale = jnp.concatenate([gain] * (width // LANES), axis=1)
        return turned(real, imag, scale * turn[row : row + 1, :], scale * turn[row + 1 : row + 2, :])

    def merge(left, right, table):
        merged = jnp.dot(table[...], joined(left, right), preferred_element_type=jnp.float32)
        return merged[:, :width], merged[:, width:]

    own, one, two, three = images
    near_turn, far_turn, last_turn = turns
    near = merge(child(own, near_turn, 0, gains[0:1]), child(one, near_turn, 2, gains[1:2]), tables[0])
    near = turned(*near, last_turn[0:1, :], last_turn[1:2, :])
    far = merge(child(two, far_turn, 0, gains[2:3]), child(three, far_turn, 2, gains[3:4]), tables[1])
    far = turned(*far, last_turn[2:3, :], last_turn[3:4, :])
    return joined(near, far)


def merge_kernel(cells, *refs):
    images, tables, turns, energies = refs[0:4], refs[4:7], refs[7:10], refs[10:14]
    result, gains = refs[14:16]

    def unsealed(tail):
        terms = tail[0].astype(jnp.float32)
        return terms[0:1] + terms[1:2] + terms[2:3]

    energy = jnp.concatenate([energies[0][...]] + [unsealed(tail) for tail in energies[1:]])
    gains[...] = lax.rsqrt(energy / cells + 1e-06)
    both = first_merges(images, tables, turns, gains[...])
    merged = jnp.dot(tables[2][...], both, preferred_element_type=jnp.float32)
    width = result.shape[-1]
    result[0, 0] = merged[:, :width].astype(jnp.bfloat16)
    result[0, 1] = merged[:, width:].astype(jnp.bfloat16)


def merge_cost(width, beams):
    flops = 8 * width * BAND * (2 * BAND + beams)
    return pl.CostEstimate(flops=flops, bytes_accessed=8192 * width, transcendentals=0)


def merge_first(images, tables, turns, energy, tails, cells, shape):
    width = images[1].shape[-1]
    beams = shape[2]
    in_specs = [pl.BlockSpec((image.shape[0], TILE, BLOCK), lambda i: (0, 0, i)) for image in images]
    in_specs += [pl.BlockSpec(t.shape, lambda i: (0, 0)) for t in tables]
    in_specs += [pl.BlockSpec((t.shape[0], BLOCK), lambda i: (0, i)) for t in turns]
    in_specs += [pl.BlockSpec((1, LANES), lambda i: (0, 0))]
    in_specs += [pl.BlockSpec((1, TILE, LANES), lambda i: (2 * SPAN, 0, 0)) for tail in tails]
    return pl.pallas_call(
        functools.partial(merge_kernel, cells),
        grid=(width // BLOCK,),
        out_shape=[jax.ShapeDtypeStruct(shape, jnp.bfloat16), jax.ShapeDtypeStruct((GROUP, LANES), jnp.float32)],
        in_specs=in_specs,
        out_specs=[
            pl.BlockSpec((1, 2, beams, BLOCK), lambda i: (0, 0, 0, i)),
            pl.BlockSpec((GROUP, LANES), lambda i: (0, 0)),
        ],
        compiler_params=pltpu.CompilerParams(vmem_limit_bytes=16 * 2**20),
        cost_estimate=merge_cost(width, beams),
        name="merge",
    )(*images, *tables, *turns, energy, *tails)


def finish_kernel(at, split, *refs):
    own, one, two, three = refs[0:split], refs[split], refs[split + 1 : 2 * split + 1], refs[2 * split + 1]
    refs = refs[2 * split + 2 :]
    tables, turns, gains = refs[0:3], refs[3:6], refs[6]
    result, buffer, sems = refs[8:11]
    width = buffer.shape[-1]
    bins = slice(at, at + width)

    def piece(parts):
        cuts, start = [], 0 if split == len(FAR_PARTS) else FAR_PARTS[0]
        for part in parts:
            size = part.shape[-1]
            low, high = max(at - start, 0), min(at + width - start, size)
            cuts.append(part[0 : 2 * SPAN, :, low:high])
            start += size
        return jnp.concatenate(cuts, axis=-1)

    images = [piece(own), one, piece(two), three]
    both = first_merges(images, tables, [turn[:, bins] for turn in turns], gains[...])
    copies = []
    for k, row in enumerate(range(0, buffer.shape[1], OUT_ROWS)):
        rows = slice(row, row + OUT_ROWS)
        merged = jnp.dot(tables[2][rows, :], both, preferred_element_type=jnp.float32)
        for half in range(2):
            buffer[half, rows] = merged[:, half * width : (half + 1) * width].astype(jnp.bfloat16)
        copies.append(pltpu.make_async_copy(buffer.at[:, rows], result.at[0, :, rows, bins], sems.at[k]))
        copies[-1].start()
    for copy in copies:
        copy.wait()


def finish(prior, at, images, tables, turns, gains):
    own, one, two, three = images
    width = one.shape[-1]
    beams = prior.shape[2]
    operands = [*own, one, *two, three, *tables, *turns, gains]
    return pl.pallas_call(
        functools.partial(finish_kernel, at, len(own)),
        out_shape=jax.ShapeDtypeStruct(prior.shape, prior.dtype),
        in_specs=[pl.BlockSpec(memory_space=pltpu.VMEM)] * len(operands) + [pl.BlockSpec(memory_space=pl.ANY)],
        out_specs=pl.BlockSpec(memory_space=pl.ANY),
        scratch_shapes=[pltpu.VMEM((2, beams, width), prior.dtype), pltpu.SemaphoreType.DMA((beams // OUT_ROWS,))],
        input_output_aliases={len(operands): 0},
        compiler_params=pltpu.CompilerParams(vmem_limit_bytes=16 * 2**20),
        cost_estimate=merge_cost(width, beams),
        name="finish",
    )(*operands, prior)


def shards(polar, autofocus, offsets, weights):
    beams, bins = polar.shape[2], polar.shape[3]
    cells = 2 * beams * lax.axis_size("sec") * bins // 2
    rows = polar.reshape(2, beams // TILE, TILE, bins)

    first = cut(rows)
    far = [partner(first, 2)]
    rows, first = lax.optimization_barrier((rows, first))
    second, *near, energy, near_data, last_data = prepare(rows, (weights, offsets, autofocus))
    energy = lax.psum(energy, "sec")
    second, near[0] = seal(second, near[0], energy)
    far.append(partner(second, 2))
    near_table, near_turn = make_table(BAND, near_data, beams)
    last_table, last_turn = make_table(beams, last_data, beams)
    near[1], far[0], near_table, last_table = lax.optimization_barrier((near[1], far[0], near_table, last_table))
    far_table, far_turn = make_table(BAND, far[1], beams)
    near[2], far_table = lax.optimization_barrier((near[2], far_table))
    one, three = ([partner(part, flip) for part in near] for flip in (1, 3))

    tables = [near_table, far_table, last_table]
    turns = [near_turn, far_turn, last_turn]
    images = [first, one[0], far[0], three[0]]
    merged, gains = merge_first(images, tables, turns, energy, [one[0], far[1], three[0]], cells, polar.shape)
    at = NEAR_PARTS[0]
    for i in (1, 2):
        k = int(at >= FAR_PARTS[0])
        merged = finish(merged, at, [(first, second)[k:], one[i], far[k:], three[i]], tables, turns, gains)
        at += NEAR_PARTS[i]
    return merged


def solution(mesh):
    ring = Mesh(mesh.devices.reshape(-1, GROUP, mesh.devices.shape[1]), ("rest", "x", "sec"))
    placed = (
        P(("rest", "x"), None, "sec", None),
        P(None, None, ("rest", "x"), None),
        P(None, None, ("rest", "x"), "sec"),
        P(None, None, ("rest", "x"), None, "sec"),
    )
    return jax.shard_map(
        shards, mesh=ring, in_specs=placed, out_specs=P(("rest", "x"), None, "sec", None), check_vma=False
    )
```

```python
import functools

import jax
import jax.numpy as jnp
from jax import lax
from jax.experimental import pallas as pl
from jax.experimental.pallas import tpu as pltpu
from jax.sharding import Mesh
from jax.sharding import PartitionSpec as P

GROUP = 4
TILE = 8
STEP = 31
SPAN = 33
BAND = SPAN * TILE
BULK = 256
TAPS = 8
LANES = 128
BLOCK = 384
OUT_ROWS = 256
FAR_PARTS = (640, 384)
NEAR_PARTS = (384, 384, 256)
DATA_TILES = 6
PIECES = 4
TERMS = 3


def partner(value, flip):
    return lax.ppermute(value, "x", [(i, i ^ flip) for i in range(GROUP)])


def terms_of(value):
    terms = []
    for _ in range(TERMS):
        terms.append(value.astype(jnp.bfloat16).astype(jnp.float32))
        value = value - terms[-1]
    return terms


def place_bits():
    place = lax.axis_index("x")
    return place % 2, place // 2


def encode(tail, bit, weights, offsets, phases):
    beams = weights.shape[-1]
    own = bit == 0
    starts, angles = [], []
    for child in range(2):
        lanes = slice(child * beams, (child + 1) * beams)
        taps = jnp.where(own, weights[child, 0], weights[1 - child, 0])
        tail[0, :, lanes] = taps.astype(jnp.bfloat16)
        start = jnp.where(own, offsets[child], offsets[1 - child]) - bit * (STEP * TILE)
        starts.append(start.astype(jnp.float32))
        angles += terms_of(jnp.where(own, phases[child], phases[1 - child]))
    rows = [jnp.concatenate(starts, axis=1)] + angles
    rows.append(jnp.zeros((TILE - len(rows), 2 * beams), jnp.float32))
    tail[1] = jnp.concatenate(rows).astype(jnp.bfloat16)


def decode(data, lanes):
    if data.shape[0] == 2:
        return data[0].astype(jnp.float32), data[1].astype(jnp.float32)
    at, each = 2 * SPAN + 1, DATA_TILES // 2
    return [
        jnp.concatenate([data[at + i * each + k].astype(jnp.float32) for k in range(each)], axis=1)[:, :lanes]
        for i in range(2)
    ]


def cut_kernel(rows, result, sems):
    low, _ = place_bits()
    copies = []
    for half in range(2):
        for i in range(PIECES):
            at, end = SPAN * i // PIECES, SPAN * (i + 1) // PIECES
            source = rows.at[half, pl.ds(low * STEP + at, end - at), :, 0 : result.shape[-1]]
            target = result.at[pl.ds(half * SPAN + at, end - at)]
            copies.append(pltpu.make_async_copy(source, target, sems.at[len(copies)]))
            copies[-1].start()
    for copy in copies:
        copy.wait()


def cut(rows):
    return pl.pallas_call(
        cut_kernel,
        out_shape=jax.ShapeDtypeStruct((2 * SPAN, TILE, FAR_PARTS[0]), rows.dtype),
        in_specs=[pl.BlockSpec(memory_space=pl.ANY)],
        out_specs=pl.BlockSpec(memory_space=pltpu.VMEM),
        scratch_shapes=[pltpu.SemaphoreType.DMA((2 * PIECES,))],
        compiler_params=pltpu.CompilerParams(vmem_limit_bytes=52 * 2**20),
        cost_estimate=pl.CostEstimate(flops=0, bytes_accessed=1_600_000, transcendentals=0),
        name="cut",
    )(rows)


def section_specs(section, *arrays):
    def spec(shape):
        return pl.BlockSpec((1, *shape[1:]), lambda i: (section,) + (0,) * (len(shape) - 1))

    return [spec(array.shape) for array in arrays]


def prepare_kernel(*refs):
    low, high = place_bits()
    sections, rows = (refs[0:3], refs[3:6]), refs[6]
    far, *near, energy, near_data, last_data, image, sems = refs[7:]
    piece = image.shape[1] // PIECES
    loads = []
    for k in range(PIECES):
        some = pl.ds(k * piece, piece)
        loads.append(pltpu.make_async_copy(rows.at[:, some], image.at[:, some], sems.at[k]))
        loads[-1].start()
    for data, bit, section in zip((near_data, last_data), (low, high), sections):
        encode(data, bit, *(array.at[0] for array in section))
    width, each = far.shape[-1], DATA_TILES // 2
    for i in range(2):
        for k in range(each):
            some = near_data[i, :, k * width : (k + 1) * width]
            far[2 * SPAN + 1 + i * each + k, :, 0 : some.shape[-1]] = some

    def add(i, total):
        block = image[:, pl.ds(i * 4, 4)].astype(jnp.float32)
        return total + jnp.sum(block * block, axis=(0, 1))

    total = jnp.zeros(image.shape[2:], jnp.float32)
    for k in range(PIECES):
        loads[k].wait()
        total = lax.fori_loop(k * piece // 4, (k + 1) * piece // 4, add, total)
    energy[...] = jnp.broadcast_to(jnp.sum(total, keepdims=True), energy.shape)
    for half in range(2):
        place = slice(half * SPAN, (half + 1) * SPAN)
        far[place] = image[half, pl.ds(low * STEP, SPAN), :, FAR_PARTS[0] :]
        at = 0
        for part in near:
            width = part.shape[-1]
            part[place] = image[half, pl.ds((1 - low) * STEP, SPAN), :, at : at + width]
            at += width


def prepare(rows, section):
    bins = rows.shape[-1]
    sizes = [(2 * SPAN + 1 + DATA_TILES, FAR_PARTS[1])] + [(2 * SPAN + (i == 0), w) for i, w in enumerate(NEAR_PARTS)]
    shapes = [jax.ShapeDtypeStruct((tiles, TILE, w), rows.dtype) for tiles, w in sizes]
    shapes.append(jax.ShapeDtypeStruct((1, LANES), jnp.float32))
    shapes += [jax.ShapeDtypeStruct((2, TILE, bins), rows.dtype)] * 2
    return pl.pallas_call(
        prepare_kernel,
        grid=(1,),
        out_shape=shapes,
        in_specs=[*section_specs(0, *section), *section_specs(1, *section), pl.BlockSpec(memory_space=pl.ANY)],
        out_specs=[pl.BlockSpec(memory_space=pltpu.VMEM)] * len(shapes),
        scratch_shapes=[pltpu.VMEM(rows.shape, rows.dtype), pltpu.SemaphoreType.DMA((PIECES,))],
        compiler_params=pltpu.CompilerParams(vmem_limit_bytes=52 * 2**20),
        cost_estimate=pl.CostEstimate(flops=4 * SPAN * TILE * bins, bytes_accessed=4_000_000, transcendentals=0),
        name="prepare",
    )(*section, *section, rows)


def seal_kernel(far, near, energy, far_result, near_result, tail, sems):
    row = lax.broadcasted_iota(jnp.int32, (TILE, LANES), 0)
    value = jnp.zeros((TILE, LANES), jnp.float32)
    for i, term in enumerate(terms_of(energy[...])):
        value = jnp.where(row == i, term, value)
    tail[0] = value.astype(jnp.bfloat16)
    copies = [
        pltpu.make_async_copy(tail, result.at[pl.ds(2 * SPAN, 1), :, 0:LANES], sems.at[i])
        for i, result in enumerate((far_result, near_result))
    ]
    for copy in copies:
        copy.start()
    for copy in copies:
        copy.wait()


def seal(far, near, energy):
    anywhere = pl.BlockSpec(memory_space=pl.ANY)
    return pl.pallas_call(
        seal_kernel,
        out_shape=[jax.ShapeDtypeStruct(part.shape, part.dtype) for part in (far, near)],
        in_specs=[anywhere, anywhere, pl.BlockSpec(memory_space=pltpu.VMEM)],
        out_specs=[anywhere, anywhere],
        scratch_shapes=[pltpu.VMEM((1, TILE, LANES), far.dtype), pltpu.SemaphoreType.DMA((2,))],
        input_output_aliases={0: 0, 1: 1},
        compiler_params=pltpu.CompilerParams(vmem_limit_bytes=4 * 2**20),
        cost_estimate=pl.CostEstimate(flops=10_000, bytes_accessed=20_000, transcendentals=0),
        name="seal",
    )(far, near, energy)


def build_table(target, columns, first_row, row_tiles, group):
    rows = group * TILE
    lane = lax.broadcasted_iota(jnp.int32, (rows, LANES), 1)

    def step(i, carry):
        block = columns[pl.ds(pl.multiple_of(first_row + i * rows, TILE), rows), :]
        place = pl.ds(pl.multiple_of(i * rows, TILE), rows)

        def spread(column):
            return jnp.broadcast_to(block[:, column : column + 1], (rows, LANES))

        rest = jnp.zeros((rows, LANES), jnp.float32)
        for child in range(2):
            start = spread(2 * TAPS + child).astype(jnp.int32)
            taps = [spread(child * TAPS + t) for t in range(TAPS)]

            def entries(source, part):
                hit = source - start
                for t in range(TAPS):
                    part = jnp.where(hit == t, taps[t], part)
                return part

            for part in range(BULK // LANES):
                at = child * BULK + part * LANES
                target[place, at : at + LANES] = entries(lane + part * LANES, jnp.zeros((rows, LANES), jnp.float32))
            inside = (lane >= child * TILE) & (lane < (child + 1) * TILE)
            rest = entries(jnp.where(inside, lane + (BULK - child * TILE), -TAPS), rest)
        target[place, 2 * BULK : 2 * BAND] = rest[:, : 2 * TILE]
        return carry

    lax.fori_loop(0, row_tiles // group, step, 0)


def table_kernel(data, table, turn, columns):
    beams = columns.shape[0]
    taps, rest = decode(data, 2 * beams)
    starts = jnp.concatenate([rest[:1, :beams], rest[:1, beams:], jnp.zeros((TILE - 2, beams), jnp.float32)])
    fill = jnp.zeros((LANES - 2 * TAPS - TILE, beams), jnp.float32)
    columns[...] = jnp.transpose(jnp.concatenate([taps[:, :beams], taps[:, beams:], starts, fill]))
    for child in range(2):
        at = 1 + child * TERMS
        phase = rest[at : at + 1] + rest[at + 1 : at + 2] + rest[at + 2 : at + 3]
        turn[2 * child : 2 * child + 1, :] = jnp.cos(phase)
        turn[2 * child + 1 : 2 * child + 2, :] = jnp.sin(phase)
    first_row = place_bits()[1] * (STEP * TILE) if table.shape[0] == BAND else 0
    row_tiles = table.shape[0] // TILE
    build_table(table, columns, first_row, row_tiles, 3 if row_tiles % 3 == 0 else 4)


def make_table(rows, data, beams):
    whole = pl.BlockSpec(memory_space=pltpu.VMEM)
    table, turn = pl.pallas_call(
        table_kernel,
        out_shape=[jax.ShapeDtypeStruct(s, jnp.float32) for s in ((rows, 2 * BAND), (4, 2 * beams))],
        in_specs=[whole],
        out_specs=[whole] * 2,
        scratch_shapes=[pltpu.VMEM((beams, LANES), jnp.float32)],
        compiler_params=pltpu.CompilerParams(vmem_limit_bytes=8 * 2**20),
        cost_estimate=pl.CostEstimate(flops=rows * 12_000, bytes_accessed=rows * 4096, transcendentals=8192),
        name="table",
    )(data)
    return table.astype(jnp.bfloat16), turn


def turned(real, imag, cosine, sine):
    return cosine * real - sine * imag, sine * real + cosine * imag


def joined(left, right):
    both = []
    for a, b in zip(left, right):
        both.append(jnp.concatenate([a[:BULK], b[:BULK], a[BULK:], b[BULK:]]).astype(jnp.bfloat16))
    return jnp.concatenate(both, axis=1)


def child(source, turn, row, gain):
    width = source.shape[-1]
    real, imag = (source[half * SPAN : (half + 1) * SPAN].astype(jnp.float32).reshape(BAND, width) for half in range(2))
    scale = jnp.concatenate([gain] * (width // LANES), axis=1)
    return turned(real, imag, scale * turn[row : row + 1, :], scale * turn[row + 1 : row + 2, :])


def halves(merged):
    width = merged.shape[1] // 2
    return merged[:, :width], merged[:, width:]


def first_merges(images, tables, turns, gains):
    def merge(left, right, table):
        return halves(jnp.dot(table[...], joined(left, right), preferred_element_type=jnp.float32))

    own, one, two, three = images
    near_turn, far_turn, last_turn = turns
    near = merge(child(own, near_turn, 0, gains[0:1]), child(one, near_turn, 2, gains[1:2]), tables[0])
    near = turned(*near, last_turn[0:1, :], last_turn[1:2, :])
    far = merge(child(two, far_turn, 0, gains[2:3]), child(three, far_turn, 2, gains[3:4]), tables[1])
    far = turned(*far, last_turn[2:3, :], last_turn[3:4, :])
    return joined(near, far)


def ready_kernel(at, own, two, near_table, far_table, near_turn, far_turn, gains, result):
    width = result.shape[-1] // 2
    skip = at - FAR_PARTS[0]
    bins = slice(at, at + width)
    pairs = ((own, near_table, near_turn, 0), (two, far_table, far_turn, 2))
    for i, (source, table, turn, k) in enumerate(pairs):
        source = source[0 : 2 * SPAN, :, skip : skip + width]
        rows = jnp.concatenate(child(source, turn[:, bins], 0, gains[k : k + 1, :]), axis=1)
        rest = jnp.concatenate([rows[BULK:], jnp.zeros((TILE, 2 * width), jnp.float32)])
        bulk = jnp.dot(table[:, 0:BULK], rows[:BULK].astype(jnp.bfloat16), preferred_element_type=jnp.float32)
        tail = jnp.dot(table[:, 2 * BULK :], rest.astype(jnp.bfloat16), preferred_element_type=jnp.float32)
        result[i] = bulk + tail


def ready(at, width, own, two, tables, turns, gains):
    operands = [own, two, *tables, *turns, gains]
    return pl.pallas_call(
        functools.partial(ready_kernel, at),
        out_shape=jax.ShapeDtypeStruct((2, BAND, 2 * width), jnp.float32),
        in_specs=[pl.BlockSpec(memory_space=pltpu.VMEM)] * len(operands),
        out_specs=pl.BlockSpec(memory_space=pltpu.VMEM),
        compiler_params=pltpu.CompilerParams(vmem_limit_bytes=12 * 2**20),
        cost_estimate=merge_cost(width, BAND),
        name="ready",
    )(*operands)


def last_kernel(at, *refs):
    made, one, three, near_table, far_table, last_table, near_turn, far_turn, last_turn, gains = refs[:10]
    result, buffer, sems = refs[11:14]
    width = buffer.shape[-1]
    bins = slice(at, at + width)

    def merge(i, source, table, turn, k):
        rows = jnp.concatenate(child(source, turn[:, bins], 2, gains[k : k + 1, :]), axis=1)
        rows = jnp.concatenate([rows[:BULK], jnp.zeros((TILE, 2 * width), jnp.float32), rows[BULK:]])
        added = jnp.dot(table[:, BULK:], rows.astype(jnp.bfloat16), preferred_element_type=jnp.float32)
        turns = last_turn[2 * i : 2 * i + 2, bins]
        return turned(*halves(made[i] + added), turns[0:1], turns[1:2])

    both = joined(merge(0, one, near_table, near_turn, 1), merge(1, three, far_table, far_turn, 3))
    write_out(both, last_table, buffer, result, bins, sems)


def write_out(both, table, buffer, result, bins, sems):
    copies = []
    for k, row in enumerate(range(0, buffer.shape[1], OUT_ROWS)):
        rows = slice(row, row + OUT_ROWS)
        merged = jnp.dot(table[rows, :], both, preferred_element_type=jnp.float32)
        for half, part in enumerate(halves(merged)):
            buffer[half, rows] = part.astype(jnp.bfloat16)
        copies.append(pltpu.make_async_copy(buffer.at[:, rows], result.at[0, :, rows, bins], sems.at[k]))
        copies[-1].start()
    for copy in copies:
        copy.wait()


def merge_kernel(cells, *refs):
    images, tables, turns, energies = refs[0:4], refs[4:7], refs[7:10], refs[10:14]
    result, gains = refs[14:16]

    def unsealed(tail):
        terms = tail[0].astype(jnp.float32)
        return terms[0:1] + terms[1:2] + terms[2:3]

    energy = jnp.concatenate([energies[0][...]] + [unsealed(tail) for tail in energies[1:]])
    gains[...] = lax.rsqrt(energy / cells + 1e-06)
    both = first_merges(images, tables, turns, gains[...])
    merged = jnp.dot(tables[2][...], both, preferred_element_type=jnp.float32)
    width = result.shape[-1]
    result[0, 0] = merged[:, :width].astype(jnp.bfloat16)
    result[0, 1] = merged[:, width:].astype(jnp.bfloat16)


def merge_cost(width, beams):
    flops = 8 * width * BAND * (2 * BAND + beams)
    return pl.CostEstimate(flops=flops, bytes_accessed=8192 * width, transcendentals=0)


def merge_first(images, tables, turns, energy, tails, cells, shape):
    width = images[1].shape[-1]
    beams = shape[2]
    in_specs = [pl.BlockSpec((image.shape[0], TILE, BLOCK), lambda i: (0, 0, i)) for image in images]
    in_specs += [pl.BlockSpec(t.shape, lambda i: (0, 0)) for t in tables]
    in_specs += [pl.BlockSpec((t.shape[0], BLOCK), lambda i: (0, i)) for t in turns]
    in_specs += [pl.BlockSpec((1, LANES), lambda i: (0, 0))]
    in_specs += [pl.BlockSpec((1, TILE, LANES), lambda i: (2 * SPAN, 0, 0)) for tail in tails]
    return pl.pallas_call(
        functools.partial(merge_kernel, cells),
        grid=(width // BLOCK,),
        out_shape=[jax.ShapeDtypeStruct(shape, jnp.bfloat16), jax.ShapeDtypeStruct((GROUP, LANES), jnp.float32)],
        in_specs=in_specs,
        out_specs=[
            pl.BlockSpec((1, 2, beams, BLOCK), lambda i: (0, 0, 0, i)),
            pl.BlockSpec((GROUP, LANES), lambda i: (0, 0)),
        ],
        compiler_params=pltpu.CompilerParams(vmem_limit_bytes=16 * 2**20),
        cost_estimate=merge_cost(width, beams),
        name="merge",
    )(*images, *tables, *turns, energy, *tails)


def finish_kernel(at, split, *refs):
    own, one, two, three = refs[0:split], refs[split], refs[split + 1 : 2 * split + 1], refs[2 * split + 1]
    refs = refs[2 * split + 2 :]
    tables, turns, gains = refs[0:3], refs[3:6], refs[6]
    result, buffer, sems = refs[8:11]
    width = buffer.shape[-1]
    bins = slice(at, at + width)

    def piece(parts):
        cuts, start = [], 0 if split == len(FAR_PARTS) else FAR_PARTS[0]
        for part in parts:
            size = part.shape[-1]
            low, high = max(at - start, 0), min(at + width - start, size)
            cuts.append(part[0 : 2 * SPAN, :, low:high])
            start += size
        return jnp.concatenate(cuts, axis=-1)

    images = [piece(own), one, piece(two), three]
    both = first_merges(images, tables, [turn[:, bins] for turn in turns], gains[...])
    write_out(both, tables[2], buffer, result, bins, sems)


def finish(kernel, prior, width, operands):
    beams = prior.shape[2]
    return pl.pallas_call(
        kernel,
        out_shape=jax.ShapeDtypeStruct(prior.shape, prior.dtype),
        in_specs=[pl.BlockSpec(memory_space=pltpu.VMEM)] * len(operands) + [pl.BlockSpec(memory_space=pl.ANY)],
        out_specs=pl.BlockSpec(memory_space=pl.ANY),
        scratch_shapes=[pltpu.VMEM((2, beams, width), prior.dtype), pltpu.SemaphoreType.DMA((beams // OUT_ROWS,))],
        input_output_aliases={len(operands): 0},
        compiler_params=pltpu.CompilerParams(vmem_limit_bytes=16 * 2**20),
        cost_estimate=merge_cost(width, beams),
        name="finish",
    )(*operands, prior)


def shards(polar, autofocus, offsets, weights):
    beams, bins = polar.shape[2], polar.shape[3]
    cells = 2 * beams * lax.axis_size("sec") * bins // 2
    rows = polar.reshape(2, beams // TILE, TILE, bins)

    first = cut(rows)
    far = [partner(first, 2)]
    rows, first = lax.optimization_barrier((rows, first))
    second, *near, energy, near_data, last_data = prepare(rows, (weights, offsets, autofocus))
    energy = lax.psum(energy, "sec")
    second, near[0] = seal(second, near[0], energy)
    far.append(partner(second, 2))
    near_table, near_turn = make_table(BAND, near_data, beams)
    last_table, last_turn = make_table(beams, last_data, beams)
    near[1], far[0], near_table, last_table = lax.optimization_barrier((near[1], far[0], near_table, last_table))
    far_table, far_turn = make_table(BAND, far[1], beams)
    near[2], far_table = lax.optimization_barrier((near[2], far_table))
    one, three = ([partner(part, flip) for part in near] for flip in (1, 3))

    tables = [near_table, far_table, last_table]
    turns = [near_turn, far_turn, last_turn]
    images = [first, one[0], far[0], three[0]]
    merged, gains = merge_first(images, tables, turns, energy, [one[0], far[1], three[0]], cells, polar.shape)
    at, width = NEAR_PARTS[:2]
    operands = [first, second, one[1], *far, three[1], *tables, *turns, gains]
    merged = finish(functools.partial(finish_kernel, at, 2), merged, width, operands)
    at, width = at + width, NEAR_PARTS[2]
    made = ready(at, width, second, far[1], tables[:2], turns[:2], gains)
    operands = [made, one[2], three[2], *tables, *turns, gains]
    return finish(functools.partial(last_kernel, at), merged, width, operands)


def solution(mesh):
    ring = Mesh(mesh.devices.reshape(-1, GROUP, mesh.devices.shape[1]), ("rest", "x", "sec"))
    placed = (
        P(("rest", "x"), None, "sec", None),
        P(None, None, ("rest", "x"), None),
        P(None, None, ("rest", "x"), "sec"),
        P(None, None, ("rest", "x"), None, "sec"),
    )
    return jax.shard_map(
        shards, mesh=ring, in_specs=placed, out_specs=P(("rest", "x"), None, "sec", None), check_vma=False
    )
```

```python
import functools

import jax
import jax.numpy as jnp
from jax import lax
from jax.experimental import pallas as pl
from jax.experimental.pallas import tpu as pltpu
from jax.sharding import Mesh
from jax.sharding import PartitionSpec as P

GROUP = 4
TILE = 8
STEP = 31
SPAN = 33
BAND = SPAN * TILE
BULK = 256
TAPS = 8
LANES = 128
BLOCK = 384
FAR_PARTS = (640, 384)
NEAR_PARTS = (384, 384, 256)
DATA_TILES = 6
PIECES = 4
TERMS = 3


def partner(value, flip):
    return lax.ppermute(value, "x", [(i, i ^ flip) for i in range(GROUP)])


def terms_of(value):
    terms = []
    for _ in range(TERMS):
        terms.append(value.astype(jnp.bfloat16).astype(jnp.float32))
        value = value - terms[-1]
    return terms


def place_bits():
    place = lax.axis_index("x")
    return place % 2, place // 2


def encode(tail, bit, weights, offsets, phases):
    beams = weights.shape[-1]
    own = bit == 0
    starts, angles = [], []
    for child in range(2):
        lanes = slice(child * beams, (child + 1) * beams)
        taps = jnp.where(own, weights[child, 0], weights[1 - child, 0])
        tail[0, :, lanes] = taps.astype(jnp.bfloat16)
        start = jnp.where(own, offsets[child], offsets[1 - child]) - bit * (STEP * TILE)
        starts.append(start.astype(jnp.float32))
        angles += terms_of(jnp.where(own, phases[child], phases[1 - child]))
    rows = [jnp.concatenate(starts, axis=1)] + angles
    rows.append(jnp.zeros((TILE - len(rows), 2 * beams), jnp.float32))
    tail[1] = jnp.concatenate(rows).astype(jnp.bfloat16)


def decode(data, lanes):
    if data.shape[0] == 2:
        return data[0].astype(jnp.float32), data[1].astype(jnp.float32)
    at, each = 2 * SPAN + 1, DATA_TILES // 2
    return [
        jnp.concatenate([data[at + i * each + k].astype(jnp.float32) for k in range(each)], axis=1)[:, :lanes]
        for i in range(2)
    ]


def cut_kernel(rows, result, sems):
    low, _ = place_bits()
    copies = []
    for half in range(2):
        for i in range(PIECES):
            at, end = SPAN * i // PIECES, SPAN * (i + 1) // PIECES
            source = rows.at[half, pl.ds(low * STEP + at, end - at), :, 0 : result.shape[-1]]
            target = result.at[pl.ds(half * SPAN + at, end - at)]
            copies.append(pltpu.make_async_copy(source, target, sems.at[len(copies)]))
            copies[-1].start()
    for copy in copies:
        copy.wait()


def cut(rows):
    return pl.pallas_call(
        cut_kernel,
        out_shape=jax.ShapeDtypeStruct((2 * SPAN, TILE, FAR_PARTS[0]), rows.dtype),
        in_specs=[pl.BlockSpec(memory_space=pl.ANY)],
        out_specs=pl.BlockSpec(memory_space=pltpu.VMEM),
        scratch_shapes=[pltpu.SemaphoreType.DMA((2 * PIECES,))],
        compiler_params=pltpu.CompilerParams(vmem_limit_bytes=52 * 2**20),
        cost_estimate=pl.CostEstimate(flops=0, bytes_accessed=1_600_000, transcendentals=0),
        name="cut",
    )(rows)


def section_specs(section, *arrays):
    def spec(shape):
        return pl.BlockSpec((1, *shape[1:]), lambda i: (section,) + (0,) * (len(shape) - 1))

    return [spec(array.shape) for array in arrays]


def prepare_kernel(*refs):
    low, high = place_bits()
    sections, rows = (refs[0:3], refs[3:6]), refs[6]
    far, *near, energy, near_data, last_data, image, sems = refs[7:]
    piece = image.shape[1] // PIECES
    loads = []
    for k in range(PIECES):
        some = pl.ds(k * piece, piece)
        loads.append(pltpu.make_async_copy(rows.at[:, some], image.at[:, some], sems.at[k]))
        loads[-1].start()
    for data, bit, section in zip((near_data, last_data), (low, high), sections):
        encode(data, bit, *(array.at[0] for array in section))
    width, each = far.shape[-1], DATA_TILES // 2
    for i in range(2):
        for k in range(each):
            some = near_data[i, :, k * width : (k + 1) * width]
            far[2 * SPAN + 1 + i * each + k, :, 0 : some.shape[-1]] = some

    def add(i, total):
        block = image[:, pl.ds(i * 4, 4)].astype(jnp.float32)
        return total + jnp.sum(block * block, axis=(0, 1))

    total = jnp.zeros(image.shape[2:], jnp.float32)
    for k in range(PIECES):
        loads[k].wait()
        total = lax.fori_loop(k * piece // 4, (k + 1) * piece // 4, add, total)
    energy[...] = jnp.broadcast_to(jnp.sum(total, keepdims=True), energy.shape)
    for half in range(2):
        place = slice(half * SPAN, (half + 1) * SPAN)
        far[place] = image[half, pl.ds(low * STEP, SPAN), :, FAR_PARTS[0] :]
        at = 0
        for part in near:
            width = part.shape[-1]
            part[place] = image[half, pl.ds((1 - low) * STEP, SPAN), :, at : at + width]
            at += width


def prepare(rows, section):
    bins = rows.shape[-1]
    sizes = [(2 * SPAN + 1 + DATA_TILES, FAR_PARTS[1])] + [(2 * SPAN + (i == 0), w) for i, w in enumerate(NEAR_PARTS)]
    shapes = [jax.ShapeDtypeStruct((tiles, TILE, w), rows.dtype) for tiles, w in sizes]
    shapes.append(jax.ShapeDtypeStruct((1, LANES), jnp.float32))
    shapes += [jax.ShapeDtypeStruct((2, TILE, bins), rows.dtype)] * 2
    return pl.pallas_call(
        prepare_kernel,
        grid=(1,),
        out_shape=shapes,
        in_specs=[*section_specs(0, *section), *section_specs(1, *section), pl.BlockSpec(memory_space=pl.ANY)],
        out_specs=[pl.BlockSpec(memory_space=pltpu.VMEM)] * len(shapes),
        scratch_shapes=[pltpu.VMEM(rows.shape, rows.dtype), pltpu.SemaphoreType.DMA((PIECES,))],
        compiler_params=pltpu.CompilerParams(vmem_limit_bytes=52 * 2**20),
        cost_estimate=pl.CostEstimate(flops=4 * SPAN * TILE * bins, bytes_accessed=4_000_000, transcendentals=0),
        name="prepare",
    )(*section, *section, rows)


def seal_kernel(far, near, energy, far_result, near_result, tail, sems):
    row = lax.broadcasted_iota(jnp.int32, (TILE, LANES), 0)
    value = jnp.zeros((TILE, LANES), jnp.float32)
    for i, term in enumerate(terms_of(energy[...])):
        value = jnp.where(row == i, term, value)
    tail[0] = value.astype(jnp.bfloat16)
    copies = [
        pltpu.make_async_copy(tail, result.at[pl.ds(2 * SPAN, 1), :, 0:LANES], sems.at[i])
        for i, result in enumerate((far_result, near_result))
    ]
    for copy in copies:
        copy.start()
    for copy in copies:
        copy.wait()


def seal(far, near, energy):
    anywhere = pl.BlockSpec(memory_space=pl.ANY)
    return pl.pallas_call(
        seal_kernel,
        out_shape=[jax.ShapeDtypeStruct(part.shape, part.dtype) for part in (far, near)],
        in_specs=[anywhere, anywhere, pl.BlockSpec(memory_space=pltpu.VMEM)],
        out_specs=[anywhere, anywhere],
        scratch_shapes=[pltpu.VMEM((1, TILE, LANES), far.dtype), pltpu.SemaphoreType.DMA((2,))],
        input_output_aliases={0: 0, 1: 1},
        compiler_params=pltpu.CompilerParams(vmem_limit_bytes=4 * 2**20),
        cost_estimate=pl.CostEstimate(flops=10_000, bytes_accessed=20_000, transcendentals=0),
        name="seal",
    )(far, near, energy)


def build_table(target, columns, first_row, row_tiles, group):
    rows = group * TILE
    lane = lax.broadcasted_iota(jnp.int32, (rows, LANES), 1)

    def step(i, carry):
        block = columns[pl.ds(pl.multiple_of(first_row + i * rows, TILE), rows), :]
        place = pl.ds(pl.multiple_of(i * rows, TILE), rows)

        def spread(column):
            return jnp.broadcast_to(block[:, column : column + 1], (rows, LANES))

        rest = jnp.zeros((rows, LANES), jnp.float32)
        for child in range(2):
            start = spread(2 * TAPS + child).astype(jnp.int32)
            taps = [spread(child * TAPS + t) for t in range(TAPS)]

            def entries(source, part):
                hit = source - start
                for t in range(TAPS):
                    part = jnp.where(hit == t, taps[t], part)
                return part

            for part in range(BULK // LANES):
                at = child * BULK + part * LANES
                target[place, at : at + LANES] = entries(lane + part * LANES, jnp.zeros((rows, LANES), jnp.float32))
            inside = (lane >= child * TILE) & (lane < (child + 1) * TILE)
            rest = entries(jnp.where(inside, lane + (BULK - child * TILE), -TAPS), rest)
        target[place, 2 * BULK : 2 * BAND] = rest[:, : 2 * TILE]
        return carry

    lax.fori_loop(0, row_tiles // group, step, 0)


def table_kernel(data, table, turn, columns):
    beams = columns.shape[0]
    taps, rest = decode(data, 2 * beams)
    starts = jnp.concatenate([rest[:1, :beams], rest[:1, beams:], jnp.zeros((TILE - 2, beams), jnp.float32)])
    fill = jnp.zeros((LANES - 2 * TAPS - TILE, beams), jnp.float32)
    columns[...] = jnp.transpose(jnp.concatenate([taps[:, :beams], taps[:, beams:], starts, fill]))
    for child in range(2):
        at = 1 + child * TERMS
        phase = rest[at : at + 1] + rest[at + 1 : at + 2] + rest[at + 2 : at + 3]
        turn[2 * child : 2 * child + 1, :] = jnp.cos(phase)
        turn[2 * child + 1 : 2 * child + 2, :] = jnp.sin(phase)
    first_row = place_bits()[1] * (STEP * TILE) if table.shape[0] == BAND else 0
    row_tiles = table.shape[0] // TILE
    build_table(table, columns, first_row, row_tiles, 3 if row_tiles % 3 == 0 else 4)


def make_table(rows, data, beams):
    whole = pl.BlockSpec(memory_space=pltpu.VMEM)
    table, turn = pl.pallas_call(
        table_kernel,
        out_shape=[jax.ShapeDtypeStruct(s, jnp.float32) for s in ((rows, 2 * BAND), (4, 2 * beams))],
        in_specs=[whole],
        out_specs=[whole] * 2,
        scratch_shapes=[pltpu.VMEM((beams, LANES), jnp.float32)],
        compiler_params=pltpu.CompilerParams(vmem_limit_bytes=8 * 2**20),
        cost_estimate=pl.CostEstimate(flops=rows * 12_000, bytes_accessed=rows * 4096, transcendentals=8192),
        name="table",
    )(data)
    return table.astype(jnp.bfloat16), turn


def turned(real, imag, cosine, sine):
    return cosine * real - sine * imag, sine * real + cosine * imag


def joined(left, right):
    both = []
    for a, b in zip(left, right):
        both.append(jnp.concatenate([a[:BULK], b[:BULK], a[BULK:], b[BULK:]]).astype(jnp.bfloat16))
    return jnp.concatenate(both, axis=1)


def child(source, turn, row, gain):
    width = source.shape[-1]
    real, imag = (source[half * SPAN : (half + 1) * SPAN].astype(jnp.float32).reshape(BAND, width) for half in range(2))
    scale = jnp.concatenate([gain] * (width // LANES), axis=1)
    return turned(real, imag, scale * turn[row : row + 1, :], scale * turn[row + 1 : row + 2, :])


def halves(merged):
    width = merged.shape[1] // 2
    return merged[:, :width], merged[:, width:]


def first_merges(images, tables, turns, gains):
    def merge(left, right, table):
        return halves(jnp.dot(table[...], joined(left, right), preferred_element_type=jnp.float32))

    own, one, two, three = images
    near_turn, far_turn, last_turn = turns
    near = merge(child(own, near_turn, 0, gains[0:1]), child(one, near_turn, 2, gains[1:2]), tables[0])
    near = turned(*near, last_turn[0:1, :], last_turn[1:2, :])
    far = merge(child(two, far_turn, 0, gains[2:3]), child(three, far_turn, 2, gains[3:4]), tables[1])
    far = turned(*far, last_turn[2:3, :], last_turn[3:4, :])
    return joined(near, far)


def ready_kernel(at, own, two, near_table, far_table, near_turn, far_turn, gains, result):
    width = result.shape[-1] // 2
    skip = at - FAR_PARTS[0]
    bins = slice(at, at + width)
    pairs = ((own, near_table, near_turn, 0), (two, far_table, far_turn, 2))
    for i, (source, table, turn, k) in enumerate(pairs):
        source = source[0 : 2 * SPAN, :, skip : skip + width]
        rows = jnp.concatenate(child(source, turn[:, bins], 0, gains[k : k + 1, :]), axis=1)
        rest = jnp.concatenate([rows[BULK:], jnp.zeros((TILE, 2 * width), jnp.float32)])
        bulk = jnp.dot(table[:, 0:BULK], rows[:BULK].astype(jnp.bfloat16), preferred_element_type=jnp.float32)
        tail = jnp.dot(table[:, 2 * BULK :], rest.astype(jnp.bfloat16), preferred_element_type=jnp.float32)
        result[i] = bulk + tail


def ready(at, width, own, two, tables, turns, gains):
    operands = [own, two, *tables, *turns, gains]
    return pl.pallas_call(
        functools.partial(ready_kernel, at),
        out_shape=jax.ShapeDtypeStruct((2, BAND, 2 * width), jnp.float32),
        in_specs=[pl.BlockSpec(memory_space=pltpu.VMEM)] * len(operands),
        out_specs=pl.BlockSpec(memory_space=pltpu.VMEM),
        compiler_params=pltpu.CompilerParams(vmem_limit_bytes=12 * 2**20),
        cost_estimate=merge_cost(width, BAND),
        name="ready",
    )(*operands)


def last_kernel(at, *refs):
    made, one, three, near_table, far_table, last_table, near_turn, far_turn, last_turn, gains = refs[:10]
    result, buffer, sems = refs[11:14]
    width = buffer.shape[-1]
    bins = slice(at, at + width)

    def merge(i, source, table, turn, k):
        rows = jnp.concatenate(child(source, turn[:, bins], 2, gains[k : k + 1, :]), axis=1)
        rows = jnp.concatenate([rows[:BULK], jnp.zeros((TILE, 2 * width), jnp.float32), rows[BULK:]])
        added = jnp.dot(table[:, BULK:], rows.astype(jnp.bfloat16), preferred_element_type=jnp.float32)
        turns = last_turn[2 * i : 2 * i + 2, bins]
        return turned(*halves(made[i] + added), turns[0:1], turns[1:2])

    both = joined(merge(0, one, near_table, near_turn, 1), merge(1, three, far_table, far_turn, 3))
    write_out(both, last_table, buffer, result, bins, sems)


def write_out(both, table, buffer, result, bins, sems):
    copies = []
    for half, part in enumerate(halves(both)):
        merged = jnp.dot(table[...], part, preferred_element_type=jnp.float32)
        buffer[half] = merged.astype(jnp.bfloat16)
        copies.append(pltpu.make_async_copy(buffer.at[half], result.at[0, half, :, bins], sems.at[half]))
        copies[-1].start()
    for copy in copies:
        copy.wait()


def merge_kernel(cells, *refs):
    images, tables, turns, energies = refs[0:4], refs[4:7], refs[7:10], refs[10:14]
    result, gains = refs[14:16]

    def unsealed(tail):
        terms = tail[0].astype(jnp.float32)
        return terms[0:1] + terms[1:2] + terms[2:3]

    energy = jnp.concatenate([energies[0][...]] + [unsealed(tail) for tail in energies[1:]])
    gains[...] = lax.rsqrt(energy / cells + 1e-06)
    both = first_merges(images, tables, turns, gains[...])
    merged = jnp.dot(tables[2][...], both, preferred_element_type=jnp.float32)
    width = result.shape[-1]
    result[0, 0] = merged[:, :width].astype(jnp.bfloat16)
    result[0, 1] = merged[:, width:].astype(jnp.bfloat16)


def merge_cost(width, beams):
    flops = 8 * width * BAND * (2 * BAND + beams)
    return pl.CostEstimate(flops=flops, bytes_accessed=8192 * width, transcendentals=0)


def merge_first(images, tables, turns, energy, tails, cells, shape):
    width = images[1].shape[-1]
    beams = shape[2]
    in_specs = [pl.BlockSpec((image.shape[0], TILE, BLOCK), lambda i: (0, 0, i)) for image in images]
    in_specs += [pl.BlockSpec(t.shape, lambda i: (0, 0)) for t in tables]
    in_specs += [pl.BlockSpec((t.shape[0], BLOCK), lambda i: (0, i)) for t in turns]
    in_specs += [pl.BlockSpec((1, LANES), lambda i: (0, 0))]
    in_specs += [pl.BlockSpec((1, TILE, LANES), lambda i: (2 * SPAN, 0, 0)) for tail in tails]
    return pl.pallas_call(
        functools.partial(merge_kernel, cells),
        grid=(width // BLOCK,),
        out_shape=[jax.ShapeDtypeStruct(shape, jnp.bfloat16), jax.ShapeDtypeStruct((GROUP, LANES), jnp.float32)],
        in_specs=in_specs,
        out_specs=[
            pl.BlockSpec((1, 2, beams, BLOCK), lambda i: (0, 0, 0, i)),
            pl.BlockSpec((GROUP, LANES), lambda i: (0, 0)),
        ],
        compiler_params=pltpu.CompilerParams(vmem_limit_bytes=16 * 2**20),
        cost_estimate=merge_cost(width, beams),
        name="merge",
    )(*images, *tables, *turns, energy, *tails)


def finish_kernel(at, split, *refs):
    own, one, two, three = refs[0:split], refs[split], refs[split + 1 : 2 * split + 1], refs[2 * split + 1]
    refs = refs[2 * split + 2 :]
    tables, turns, gains = refs[0:3], refs[3:6], refs[6]
    result, buffer, sems = refs[8:11]
    width = buffer.shape[-1]
    bins = slice(at, at + width)

    def piece(parts):
        cuts, start = [], 0 if split == len(FAR_PARTS) else FAR_PARTS[0]
        for part in parts:
            size = part.shape[-1]
            low, high = max(at - start, 0), min(at + width - start, size)
            cuts.append(part[0 : 2 * SPAN, :, low:high])
            start += size
        return jnp.concatenate(cuts, axis=-1)

    images = [piece(own), one, piece(two), three]
    both = first_merges(images, tables, [turn[:, bins] for turn in turns], gains[...])
    write_out(both, tables[2], buffer, result, bins, sems)


def finish(kernel, prior, width, operands):
    beams = prior.shape[2]
    return pl.pallas_call(
        kernel,
        out_shape=jax.ShapeDtypeStruct(prior.shape, prior.dtype),
        in_specs=[pl.BlockSpec(memory_space=pltpu.VMEM)] * len(operands) + [pl.BlockSpec(memory_space=pl.ANY)],
        out_specs=pl.BlockSpec(memory_space=pl.ANY),
        scratch_shapes=[pltpu.VMEM((2, beams, width), prior.dtype), pltpu.SemaphoreType.DMA((2,))],
        input_output_aliases={len(operands): 0},
        compiler_params=pltpu.CompilerParams(vmem_limit_bytes=16 * 2**20),
        cost_estimate=merge_cost(width, beams),
        name="finish",
    )(*operands, prior)


def shards(polar, autofocus, offsets, weights):
    beams, bins = polar.shape[2], polar.shape[3]
    cells = 2 * beams * lax.axis_size("sec") * bins // 2
    rows = polar.reshape(2, beams // TILE, TILE, bins)

    first = cut(rows)
    far = [partner(first, 2)]
    rows, first = lax.optimization_barrier((rows, first))
    second, *near, energy, near_data, last_data = prepare(rows, (weights, offsets, autofocus))
    energy = lax.psum(energy, "sec")
    second, near[0] = seal(second, near[0], energy)
    far.append(partner(second, 2))
    near_table, near_turn = make_table(BAND, near_data, beams)
    last_table, last_turn = make_table(beams, last_data, beams)
    near[1], far[0], near_table, last_table = lax.optimization_barrier((near[1], far[0], near_table, last_table))
    far_table, far_turn = make_table(BAND, far[1], beams)
    near[2], far_table = lax.optimization_barrier((near[2], far_table))
    one, three = ([partner(part, flip) for part in near] for flip in (1, 3))

    tables = [near_table, far_table, last_table]
    turns = [near_turn, far_turn, last_turn]
    images = [first, one[0], far[0], three[0]]
    merged, gains = merge_first(images, tables, turns, energy, [one[0], far[1], three[0]], cells, polar.shape)
    at, width = NEAR_PARTS[:2]
    operands = [first, second, one[1], *far, three[1], *tables, *turns, gains]
    merged = finish(functools.partial(finish_kernel, at, 2), merged, width, operands)
    at, width = at + width, NEAR_PARTS[2]
    made = ready(at, width, second, far[1], tables[:2], turns[:2], gains)
    operands = [made, one[2], three[2], *tables, *turns, gains]
    return finish(functools.partial(last_kernel, at), merged, width, operands)


def solution(mesh):
    ring = Mesh(mesh.devices.reshape(-1, GROUP, mesh.devices.shape[1]), ("rest", "x", "sec"))
    placed = (
        P(("rest", "x"), None, "sec", None),
        P(None, None, ("rest", "x"), None),
        P(None, None, ("rest", "x"), "sec"),
        P(None, None, ("rest", "x"), None, "sec"),
    )
    return jax.shard_map(
        shards, mesh=ring, in_specs=placed, out_specs=P(("rest", "x"), None, "sec", None), check_vma=False
    )
```
